512 devices in a mesh: blk: 32 (over x, y_lo, core), dp: 16 (over y_hi, z).
Axes of the slice: x: 4, y: 8 (y_hi: 2, y_lo: 4; y = y_hi * 4 + y_lo), z: 8, core: 2. Of those that a mesh axis runs over, the one named last changes fastest.
Arguments:
- image_emb: bfloat16 [16384, 1024], P(('blk', 'dp')), may hold values from -4 to 4
- text_emb: bfloat16 [16384, 1024], P(('blk', 'dp')), may hold values from -4 to 4
- labels: int32 [16384], P(('blk', 'dp')), may hold values from 0 to 16383, as said below
- logit_scale: float32 [], replicated, may hold values from 8 to 30
Outputs:
- grad_image: bfloat16 [16384, 1024], P(('blk', 'dp'))
- grad_text: bfloat16 [16384, 1024], P(('blk', 'dp'))
The draws below stay inside these ranges and needn't reach their ends.
Inputs may be any that keep to these rules, and one draw needn't show every extreme that they name: labels is a permutation of 0 to 16383: the positive text of image i is text labels[i].
All inputs are finite; a program needn't handle non-finite values.
Results may differ from the reference program's by a relative error of at most 0.0085.
Values may be sent and summed in bfloat16 or wider, within the bound.
A program may use at most 64 MiB of HBM per device.

```python
import math
import jax
import jax.numpy as jnp
from jax import lax

E = 1024
B = 16384


def paired_embeddings(key, shared_weight, scale_low, scale_high, lift_rows):
    shuffled = jax.random.permutation(jax.random.fold_in(key, 11), B).astype(jnp.int32)
    common = jax.random.truncated_normal(jax.random.fold_in(key, 12), -4.0, 4.0, (B, E), jnp.float32)
    noise = jax.random.truncated_normal(jax.random.fold_in(key, 13), -4.0, 4.0, (B, E), jnp.float32)
    log_scale = jax.random.uniform(jax.random.fold_in(key, 14), (B, 1), jnp.float32, math.log(scale_low), math.log(scale_high))
    owner_of = jnp.argsort(shuffled, stable=True)
    aligned_text = (owner_of % 2048 == 7).astype(jnp.float32)[:, None]
    text_scale = jnp.exp(log_scale) * (1.0 - lift_rows * aligned_text)
    other_weight = math.sqrt(1.0 - shared_weight * shared_weight)
    text_values = text_scale * (shared_weight * common + other_weight * noise) / math.sqrt(E)
    text_values = jnp.clip(text_values, -4.0, 4.0)
    return (shuffled, common, text_values)


def draw_labels(key, part):
    base_key = key
    shuffled, common, text_values = paired_embeddings(base_key, 0.5, 0.5, 5.0, 0.0)
    return shuffled


def draw_text_emb(key, part):
    base_key = key
    shuffled, common, text_values = paired_embeddings(base_key, 0.5, 0.5, 5.0, 0.0)
    return text_values.astype(jnp.bfloat16)


def draw_image_emb(key, part):
    base_key = key
    key = jax.random.fold_in(key, 3)
    shared_weight, scale_low, scale_high = (0.5, 0.5, 5.0)
    shuffled, common, text_values = paired_embeddings(base_key, 0.5, 0.5, 5.0, 0.0)
    noise = jax.random.truncated_normal(jax.random.fold_in(key, 5), -4.0, 4.0, (B, E), jnp.float32)
    log_scale = jax.random.uniform(jax.random.fold_in(key, 6), (B, 1), jnp.float32, math.log(scale_low), math.log(scale_high))
    other_weight = math.sqrt(1.0 - shared_weight * shared_weight)
    image_values = jnp.exp(log_scale) * (shared_weight * common[shuffled] + other_weight * noise) / math.sqrt(E)
    return jnp.clip(image_values, -4.0, 4.0).astype(jnp.bfloat16)


def setup_inputs(seed: int = 0) -> dict:
    arg_keys = jax.random.split(jax.random.key(seed), 5)
    image_emb = draw_image_emb(jax.random.fold_in(arg_keys[4], 71), 0)
    text_emb = draw_text_emb(jax.random.fold_in(arg_keys[4], 71), 0)
    labels = draw_labels(jax.random.fold_in(arg_keys[4], 71), 0)
    logit_scale = jnp.clip(jnp.exp(jax.random.uniform(arg_keys[3], (), jnp.float32, math.log(8.0), math.log(30.0))), 8.0, 30.0)
    return {"image_emb": image_emb, "text_emb": text_emb, "labels": labels, "logit_scale": logit_scale}


def reference(image_emb, text_emb, labels, logit_scale):
    total_rows = image_emb.shape[0]
    width = image_emb.shape[1]
    row_block = min(512, total_rows)
    block_count = total_rows // row_block
    image_blocks = image_emb.reshape(block_count, row_block, width)
    label_blocks = labels.reshape(block_count, row_block)

    def block_logits(image_rows):
        return logit_scale * jnp.dot(image_rows, text_emb.T, preferred_element_type=jnp.float32)

    def first_pass(carry, image_rows):
        column_max, column_total = carry
        logits = block_logits(image_rows)
        row_max = jnp.max(logits, axis=1)
        row_lse = row_max + jnp.log(jnp.sum(jnp.exp(logits - row_max[:, None]), axis=1))
        new_max = jnp.maximum(column_max, jnp.max(logits, axis=0))
        column_total = column_total * jnp.exp(column_max - new_max) + jnp.sum(jnp.exp(logits - new_max[None, :]), axis=0)
        return (new_max, column_total), row_lse

    start_carry = (jnp.full((total_rows,), -jnp.inf, jnp.float32), jnp.zeros((total_rows,), jnp.float32))
    (column_max, column_total), row_lse = lax.scan(first_pass, start_carry, image_blocks)
    column_lse = column_max + jnp.log(column_total)
    column_ids = jnp.arange(total_rows, dtype=jnp.int32)

    def second_pass(text_grad, inputs):
        image_rows, row_labels, row_lse_block = inputs
        logits = block_logits(image_rows)
        target = (row_labels[:, None] == column_ids[None, :]).astype(jnp.float32)
        weights = ((jnp.exp(logits - row_lse_block[:, None]) + jnp.exp(logits - column_lse[None, :]) - 2.0 * target) * 0.5).astype(jnp.bfloat16)
        image_grad = (logit_scale * jnp.dot(weights, text_emb, preferred_element_type=jnp.float32)).astype(jnp.bfloat16)
        text_grad = text_grad + jnp.dot(weights.T, image_rows, preferred_element_type=jnp.float32)
        return text_grad, image_grad

    text_grad, image_grads = lax.scan(second_pass, jnp.zeros((total_rows, width), jnp.float32), (image_blocks, label_blocks, row_lse))
    return image_grads.reshape(total_rows, width), (logit_scale * text_grad).astype(jnp.bfloat16)
```

```python
import jax
import jax.numpy as jnp
from jax import lax
from jax.experimental import pallas as pl
from jax.experimental.pallas import tpu as pltpu
from jax.sharding import PartitionSpec as P

R = 32
E = 1024
W = E + 128
RING = 8
HALF = RING * 2 * R
SIGNS = (1, -1)
F32 = jnp.float32
BF16 = jnp.bfloat16


def hops(d, q):
    return 4 if d == q else 3


def lse2(a, b):
    top = jnp.maximum(a, b)
    return top + jnp.log(jnp.exp(a - top) + jnp.exp(b - top))


def rows_at(slot, count=R):
    return pl.ds(pl.multiple_of(slot * R, R), count)


def kernel(
    image_ref, text_ref, label_ref, scale_ref, out_image_ref, out_text_ref,
    images, texts, logits, wts, wts_t, grad_i, grad_t, row_stat, col_stat,
    row_vec, row_pair, row_ring, col_vec, col_pair, col_ring,
    swap_out, swap_in, stage, landed, last_out, last_in,
    pair_send, pair_recv, ring_send, ring_recv, sib_send, sib_recv,
    stat_send, stat_recv, srow_send, srow_recv, scol_send, scol_recv,
    swap_send, swap_recv, rs_send, rs_recv, last_send, last_recv,
):
    blk, dp = lax.axis_index("blk"), lax.axis_index("dp")
    core, x = blk % 2, blk // 8
    y, z = (dp // 8) * 4 + (blk // 2) % 4, dp % 8
    p = x % 2
    xa = x + 1 - 2 * p
    xb = (x + 2 * p + 3) % 4

    def at(x=x, y=y, z=z, core=core):
        return {"blk": (x * 4 + y % 4) * 2 + core, "dp": (y // 4) * 8 + z}

    def up(v, k):
        return (v + k + RING) % RING

    image_pair, text_pair, sibling = at(x=xa), at(x=xb), at(core=1 - core)
    diagonal = at(x=xb, core=1 - core)
    z_peers = [at(z=up(z, k)) for k in range(1, RING)]
    y_peers = [at(y=up(y, k)) for k in range(1, RING)]
    peers = [image_pair, text_pair, sibling, diagonal] + z_peers + y_peers

    barrier = pltpu.get_barrier_semaphore()
    for peer in peers:
        pl.semaphore_signal(barrier, inc=1, device_id=peer, device_id_type=pl.DeviceIdType.MESH)
    pl.semaphore_wait(barrier, len(peers))

    sent = []

    def copy(src, dst, ssem, rsem, peer):
        return pltpu.make_async_remote_copy(
            src_ref=src, dst_ref=dst, send_sem=ssem, recv_sem=rsem,
            device_id=peer, device_id_type=pl.DeviceIdType.MESH,
        )

    def send(src, dst, ssem, rsem, peer):
        one = copy(src, dst, ssem, rsem, peer)
        one.start()
        sent.append(one)

    def arrived(dst, ssem, rsem, peer):
        copy(dst, dst, ssem, rsem, peer).wait_recv()

    place, pair = (z, y), (image_pair, text_pair)
    ahead = [[at(z=up(z, s)) for s in SIGNS], [at(y=up(y, s)) for s in SIGNS]]

    def shard(kind, where, q):
        slot = where * 2 + (p if q == 0 else 1 - p)
        return (images if kind == 0 else texts).at[rows_at(slot)]

    def to_pair(kind):
        own = shard(kind, place[kind], 0)
        send(own, own, pair_send.at[kind], pair_recv.at[kind], pair[kind])

    def to_ring(kind, d, q, k):
        part = shard(kind, up(place[kind], -SIGNS[d] * (k - 1)), q)
        send(part, part, ring_send.at[kind, d, q, k - 1], ring_recv.at[kind, d, q, k - 1], ahead[kind][d])

    def sibling_slots(where, q):
        slot = where * 2 + (p if q == 0 else 1 - p)
        return texts.at[rows_at(slot)], texts.at[rows_at(slot + 2 * RING)]

    def to_sibling(step, where, q):
        mine, theirs = sibling_slots(where, q)
        send(mine, theirs, sib_send.at[q, step], sib_recv.at[q, step], sibling)

    digits = jnp.zeros((R, 128), jnp.int32)
    row_of = lax.broadcasted_iota(jnp.int32, (R, 128), 0)
    for r in range(R):
        digits = jnp.where(row_of == r, label_ref[r], digits)
    lane = lax.broadcasted_iota(jnp.int32, (R, 128), 1)
    digits = jnp.where(lane < 64, digits >> 7, digits & 127)
    own_image = rows_at(z * 2 + p)
    images[own_image, :E] = image_ref[...]
    images[own_image, E:] = digits.astype(F32).astype(BF16)
    texts[rows_at(y * 2 + p), :] = text_ref[...]

    for kind in range(2):
        for d in range(2):
            to_ring(kind, d, 0, 1)
        to_pair(kind)
    to_sibling(0, y, 0)
    for kind in range(2):
        arrived(shard(kind, place[kind], 1), pair_send.at[kind], pair_recv.at[kind], pair[kind])
        for d in range(2):
            to_ring(kind, d, 1, 1)
    to_sibling(0, y, 1)
    order = [(0, 0), (1, 0), (0, 1), (1, 1)]
    for k in range(1, 5):
        for d, q in order:
            if k > hops(d, q):
                continue
            for kind in range(2):
                where = up(place[kind], -SIGNS[d] * k)
                arrived(
                    shard(kind, where, q), ring_send.at[kind, d, q, k - 1],
                    ring_recv.at[kind, d, q, k - 1], ahead[kind][d],
                )
                if k < hops(d, q):
                    to_ring(kind, d, q, k + 1)
                if kind == 1:
                    to_sibling(k if d == 0 else RING - k, where, q)
    for q in range(2):
        for step in range(RING):
            arrived(sibling_slots(up(y, -step), q)[1], sib_send.at[q, step], sib_recv.at[q, step], sibling)

    scale = scale_ref[0]

    @pl.loop(0, 4)
    def _(n):
        cols = pl.ds(pl.multiple_of(n * 256, 256), 256)
        tile = scale * lax.dot_general(
            images[:, :E], texts[cols, :], (((1,), (1,)), ((), ())), preferred_element_type=F32
        )
        logits[:, cols] = tile
        top = jnp.max(tile, axis=0, keepdims=True)
        total = jnp.sum(jnp.exp(tile - top), axis=0, keepdims=True)
        col_vec[:, cols] = top + jnp.log(total)

    @pl.loop(0, 8)
    def _(n):
        rows = pl.ds(pl.multiple_of(n * 64, 64), 64)
        tile = logits[rows, :]
        top = jnp.max(tile, axis=1, keepdims=True)
        total = jnp.sum(jnp.exp(tile - top), axis=1, keepdims=True)
        row_stat[rows, :] = jnp.broadcast_to(top + jnp.log(total), (64, 128))

    row_vec[...] = jnp.transpose(row_stat[...])[0:1, :]

    send(row_vec, row_pair, stat_send.at[0], stat_recv.at[0], image_pair)
    col_peers = [text_pair, sibling, diagonal]
    for i, peer in enumerate(col_peers):
        send(col_vec, col_pair.at[i], stat_send.at[i + 1], stat_recv.at[i + 1], peer)
    arrived(row_pair, stat_send.at[0], stat_recv.at[0], image_pair)
    row_ring[0] = lse2(row_vec[...], row_pair[...])
    for k in range(1, RING):
        send(row_ring.at[0], row_ring.at[k], srow_send.at[k], srow_recv.at[k], z_peers[k - 1])
    for i, peer in enumerate(col_peers):
        arrived(col_pair.at[i], stat_send.at[i + 1], stat_recv.at[i + 1], peer)
    same = lse2(col_vec[...], col_pair[0])
    other = lse2(col_pair[1], col_pair[2])
    other = jnp.concatenate([other[:, HALF:], other[:, :HALF]], axis=1)
    col_ring[0] = lse2(same, other)
    for k in range(1, RING):
        send(col_ring.at[0], col_ring.at[k], scol_send.at[k], scol_recv.at[k], y_peers[k - 1])
    for k in range(1, RING):
        arrived(row_ring.at[k], srow_send.at[k], srow_recv.at[k], z_peers[k - 1])

    def joined(ring):
        parts = [ring[k] for k in range(RING)]
        top = parts[0]
        for part in parts[1:]:
            top = jnp.maximum(top, part)
        total = jnp.exp(parts[0] - top)
        for part in parts[1:]:
            total = total + jnp.exp(part - top)
        return top + jnp.log(total)

    row_stat[...] = jnp.transpose(jnp.broadcast_to(joined(row_ring), (128, HALF)))
    for k in range(1, RING):
        arrived(col_ring.at[k], scol_send.at[k], scol_recv.at[k], y_peers[k - 1])
    col_stat[...] = joined(col_ring)

    @pl.loop(0, 4)
    def _(n):
        rows = pl.ds(pl.multiple_of(n * 128, 128), 128)
        at_lane = lax.broadcasted_iota(jnp.int32, (1, 2 * HALF), 1)
        member = (at_lane >> 5) & 15
        along, parity = member >> 1, member & 1
        its_core = jnp.where(at_lane < HALF, core, 1 - core)
        its_x = jnp.where(parity == p, x, xb)
        its_blk = (its_x * 4 + (along & 3)) * 2 + its_core
        its_dp = (along >> 2) * 8 + z
        ids = ((its_blk * 16 + its_dp) * R + (at_lane & 31)).astype(F32)
        digit = images[rows, E:].astype(F32)
        label = digit[:, 0:1] * 128.0 + digit[:, 64:65]
        tile = logits[rows, :]
        target = jnp.where(label == ids, 2.0, 0.0)
        both = jnp.exp(tile - row_stat[rows, 0:1]) + jnp.exp(tile - col_stat[...])
        weight = (both - target) * 0.5
        wts[rows, :] = weight.astype(BF16)
        wts_t[:, rows] = jnp.transpose(weight).astype(BF16)

    for n in range(4):
        cols = pl.ds(n * 256, 256)
        swap_out[:, cols] = jnp.dot(
            wts_t[HALF:, :], images[:, cols], preferred_element_type=F32
        ).astype(BF16)
        send(swap_out.at[:, cols], swap_in.at[:, cols], swap_send.at[n], swap_recv.at[n], sibling)

    @pl.loop(0, 4)
    def _(n):
        cols = pl.ds(pl.multiple_of(n * 256, 256), 256)
        grad_i[:, cols] = jnp.dot(wts[...], texts[:, cols], preferred_element_type=F32)

    def own_term(kind, where, q):
        slot = where * 2 + (p if q == 0 else 1 - p)
        return (grad_i if kind == 0 else grad_t)[rows_at(slot), :]

    def pass_on(kind, d, q, s):
        term = own_term(kind, up(place[kind], SIGNS[d] * (hops(d, q) - s)), q)
        if s > 0:
            came = landed.at[kind, d, q, s - 1]
            arrived(came, rs_send.at[kind, d, q, s - 1], rs_recv.at[kind, d, q, s - 1], ahead[kind][d])
            term = term + came[...].astype(F32)
        stage[kind, d, q, s] = term.astype(BF16)
        send(
            stage.at[kind, d, q, s], landed.at[kind, d, q, s],
            rs_send.at[kind, d, q, s], rs_recv.at[kind, d, q, s], ahead[kind][d],
        )

    for d, q in order:
        pass_on(0, d, q, 0)

    @pl.loop(0, 4)
    def _(n):
        cols = pl.ds(pl.multiple_of(n * 256, 256), 256)
        grad_t[:, cols] = jnp.dot(wts_t[:HALF, :], images[:, cols], preferred_element_type=F32)

    for n in range(4):
        cols = pl.ds(n * 256, 256)
        arrived(swap_in.at[:, cols], swap_send.at[n], swap_recv.at[n], sibling)
    grad_t[...] = grad_t[...] + swap_in[...].astype(F32)
    for d, q in order:
        pass_on(1, d, q, 0)
    for s in range(1, 4):
        for kind in range(2):
            for d, q in order:
                if s < hops(d, q):
                    pass_on(kind, d, q, s)

    def complete(kind, q):
        total = own_term(kind, place[kind], q)
        for d in range(2):
            s = hops(d, q) - 1
            came = landed.at[kind, d, q, s]
            arrived(came, rs_send.at[kind, d, q, s], rs_recv.at[kind, d, q, s], ahead[kind][d])
            total = total + came[...].astype(F32)
        return total

    for kind in range(2):
        last_out[kind] = complete(kind, 1).astype(BF16)
        send(last_out.at[kind], last_in.at[kind], last_send.at[kind], last_recv.at[kind], pair[kind])
    for kind, out_ref in ((0, out_image_ref), (1, out_text_ref)):
        total = complete(kind, 0)
        arrived(last_in.at[kind], last_send.at[kind], last_recv.at[kind], pair[kind])
        out_ref[...] = (scale * (total + last_in[kind].astype(F32))).astype(BF16)

    for one in sent:
        one.wait_send()


def per_device(image_emb, text_emb, labels, logit_scale):
    vmem = pl.BlockSpec(memory_space=pltpu.VMEM)
    smem = pl.BlockSpec(memory_space=pltpu.SMEM)
    dma = pltpu.SemaphoreType.DMA
    out = jax.ShapeDtypeStruct((R, E), BF16)
    return pl.pallas_call(
        kernel,
        out_shape=(out, out),
        in_specs=[vmem, vmem, smem, smem],
        out_specs=(vmem, vmem),
        scratch_shapes=[
            pltpu.VMEM((HALF, W), BF16),
            pltpu.VMEM((2 * HALF, E), BF16),
            pltpu.VMEM((HALF, 2 * HALF), F32),
            pltpu.VMEM((HALF, 2 * HALF), BF16),
            pltpu.VMEM((2 * HALF, HALF), BF16),
            pltpu.VMEM((HALF, E), F32),
            pltpu.VMEM((HALF, E), F32),
            pltpu.VMEM((HALF, 128), F32),
            pltpu.VMEM((1, 2 * HALF), F32),
            pltpu.VMEM((1, HALF), F32),
            pltpu.VMEM((1, HALF), F32),
            pltpu.VMEM((RING, 1, HALF), F32),
            pltpu.VMEM((1, 2 * HALF), F32),
            pltpu.VMEM((3, 1, 2 * HALF), F32),
            pltpu.VMEM((RING, 1, 2 * HALF), F32),
            pltpu.VMEM((HALF, E), BF16),
            pltpu.VMEM((HALF, E), BF16),
            pltpu.VMEM((2, 2, 2, 4, R, E), BF16),
            pltpu.VMEM((2, 2, 2, 4, R, E), BF16),
            pltpu.VMEM((2, R, E), BF16),
            pltpu.VMEM((2, R, E), BF16),
            dma((2,)), dma((2,)),
            dma((2, 2, 2, 4)), dma((2, 2, 2, 4)),
            dma((2, RING)), dma((2, RING)),
            dma((4,)), dma((4,)),
            dma((RING,)), dma((RING,)),
            dma((RING,)), dma((RING,)),
            dma((4,)), dma((4,)),
            dma((2, 2, 2, 4)), dma((2, 2, 2, 4)),
            dma((2,)), dma((2,)),
        ],
        compiler_params=pltpu.CompilerParams(
            collective_id=0, has_side_effects=True, vmem_limit_bytes=40 * 1024 * 1024
        ),
        cost_estimate=pl.CostEstimate(flops=3221225472, bytes_accessed=262144, transcendentals=2097152),
        name="contrastive",
    )(image_emb, text_emb, labels, logit_scale.reshape(1))


def solution(mesh):
    in_specs = (P(("blk", "dp"), None), P(("blk", "dp"), None), P(("blk", "dp")), P())
    out_specs = (P(("blk", "dp"), None), P(("blk", "dp"), None))
    return jax.shard_map(
        per_device, mesh=mesh, in_specs=in_specs, out_specs=out_specs, check_vma=False
    )
```

```python
import jax
import jax.numpy as jnp
from jax import lax
from jax.experimental import pallas as pl
from jax.experimental.pallas import tpu as pltpu
from jax.sharding import PartitionSpec as P

R = 32
H = R // 2
E = 1024
W = E + 128
RING = 8
HALF = RING * 2 * R
GROUP = 2 * RING
F32 = jnp.float32
BF16 = jnp.bfloat16
MESH = pl.DeviceIdType.MESH

STAGES = (
    ((1, 0, 0), (0, 1, 2), (0, 1, -2), (0, 0, 1), (0, 0, -1), (0, 1, 1), (0, 1, -1), (1, 1, 0)),
    (
        (1, 0, 2), (1, 0, -2), (0, 1, 4), (0, 1, 3), (0, 1, -3), (0, 0, 2), (0, 0, -2),
        (1, 0, 1), (1, 0, -1), (1, 1, 2), (1, 1, -2), (1, 1, 1), (1, 1, -1),
    ),
    (
        (0, 0, 4), (0, 0, 3), (0, 0, -3), (1, 0, 4), (1, 0, 3), (1, 0, -3),
        (1, 1, 4), (1, 1, 3), (1, 1, -3),
    ),
)


def parent(piece):
    q, h, d = piece
    if q == 1 and (h == 1 or d == 0):
        return (0, h, d), 0
    if d == 4:
        step = -2 if (q, h) == (0, 1) else 2
        return (q, h, step), step
    step = d if abs(d) == 2 and q != h else (1 if d > 0 else -1)
    return (q, h, d - step), step


CHILDREN = {}
for _stage in STAGES:
    for _piece in _stage:
        CHILDREN.setdefault(parent(_piece)[0], []).append(_piece)
BACKWARDS = [_piece for _stage in STAGES[::-1] for _piece in _stage]


def lse2(a, b):
    top = jnp.maximum(a, b)
    return top + jnp.log(jnp.exp(a - top) + jnp.exp(b - top))


def kernel(
    image_ref, text_ref, label_ref, scale_ref, out_image_ref, out_text_ref,
    images, texts, logits, wts, wts_t, grad_i, grad_t, row_stat, col_stat,
    row_ring, col_vec, col_sib, col_ring, labels,
    swap_out, swap_in, stage, landed,
    load_sem, ring_send, ring_recv, sib_send, sib_recv, stat_send, stat_recv,
    srow_send, srow_recv, scol_send, scol_recv, swap_send, swap_recv, rs_send, rs_recv,
):
    blk, dp = lax.axis_index("blk"), lax.axis_index("dp")
    core, x = blk % 2, blk // 8
    y, z = (dp // 8) * 4 + (blk // 2) % 4, dp % 8
    p = x % 2
    xa = x + 1 - 2 * p
    xb = (x + 2 * p + 3) % 4
    sense = 1 - 2 * core

    def at(x=x, y=y, z=z, core=core):
        return {"blk": (x * 4 + y % 4) * 2 + core, "dp": (y // 4) * 8 + z}

    def along(v, d):
        return (v + sense * d + RING) % RING

    sibling = at(core=1 - core)
    image_peers = [at(x=x if q == 0 else xa, z=along(z, k)) for q in range(2) for k in range(RING)]
    text_peers = [at(x=x if q == 0 else xb, y=along(y, k)) for q in range(2) for k in range(RING)]

    own_image = pl.ds(pl.multiple_of((z * 2 + p) * R, R), R)
    own_text = pl.ds(pl.multiple_of((y * 2 + p) * R, R), R)
    loads = [
        pltpu.make_async_copy(label_ref, labels, load_sem.at[0]),
        pltpu.make_async_copy(image_ref, images.at[own_image, pl.ds(0, E)], load_sem.at[1]),
        pltpu.make_async_copy(text_ref, texts.at[own_text], load_sem.at[2]),
    ]
    for load in loads:
        load.start()
    barrier = pltpu.get_barrier_semaphore()
    steps = (1, RING - 1, 2, RING - 2, RING)
    peers = [sibling] + [image_peers[k] for k in steps] + [text_peers[k] for k in steps]
    for peer in peers:
        pl.semaphore_signal(barrier, inc=1, device_id=peer, device_id_type=MESH)
    loads[0].wait()
    digits = jnp.zeros((R, 128), jnp.int32)
    row_of = lax.broadcasted_iota(jnp.int32, (R, 128), 0)
    for r in range(R):
        digits = jnp.where(row_of == r, labels[r], digits)
    lane = lax.broadcasted_iota(jnp.int32, (R, 128), 1)
    digits = jnp.where(lane < 64, digits >> 7, digits & 127)
    images[own_image, E:] = digits.astype(F32).astype(BF16)
    loads[1].wait()
    loads[2].wait()
    pl.semaphore_wait(barrier, len(peers))

    sent = []

    def copy(src, dst, ssem, rsem, peer):
        return pltpu.make_async_remote_copy(
            src_ref=src, dst_ref=dst, send_sem=ssem, recv_sem=rsem, device_id=peer, device_id_type=MESH
        )

    def send(src, dst, ssem, rsem, peer):
        one = copy(src, dst, ssem, rsem, peer)
        one.start()
        sent.append(one)

    def arrived(dst, ssem, rsem, peer):
        copy(dst, dst, ssem, rsem, peer).wait_recv()

    place = (z, y)

    def peer_of(kind, step):
        if step == 0:
            return at(x=xa) if kind == 0 else at(x=xb)
        return at(z=along(z, step)) if kind == 0 else at(y=along(y, step))

    def piece_rows(kind, piece):
        q, h, d = piece
        slot = along(place[kind], -d) * 2 + (p if q == 0 else 1 - p)
        return pl.ds(pl.multiple_of(slot * R + h * H, H), H)

    def held(kind, piece):
        return (images if kind == 0 else texts).at[piece_rows(kind, piece)]

    def index(kind, piece):
        q, h, d = piece
        return kind, q, h, d + 3

    def gather_send(kind, piece):
        source, step = parent(piece)
        part, i = held(kind, source), index(kind, piece)
        send(part, part, ring_send.at[i], ring_recv.at[i], peer_of(kind, step))

    def sibling_rows(q, d):
        slot = along(y, -d) * 2 + (p if q == 0 else 1 - p)
        return pl.ds(pl.multiple_of(slot * R, R), R), pl.ds(pl.multiple_of(slot * R + HALF, R), R)

    def theirs(q, d):
        return sibling_rows(q, d)[1], (q, d + 3)

    def to_sibling(q, d):
        mine, there = sibling_rows(q, d)
        i = (q, (d if d == 4 else -d) + 3)
        send(texts.at[mine], texts.at[there], sib_send.at[i], sib_recv.at[i], sibling)

    for piece in STAGES[0]:
        for kind in range(2):
            gather_send(kind, piece)
    to_sibling(0, 0)
    got = set()
    for pieces in STAGES:
        for piece in pieces:
            q, h, d = piece
            for kind in (1, 0):
                i = index(kind, piece)
                arrived(held(kind, piece), ring_send.at[i], ring_recv.at[i], peer_of(kind, 0))
                for child in CHILDREN.get(piece, ()):
                    gather_send(kind, child)
            got.add(piece)
            if (q, 0, d) in got and (q, 1, d) in got:
                to_sibling(q, d)

    scale = scale_ref[0]

    def logits_of(n):
        cols = pl.ds(pl.multiple_of(n * 256, 256), 256)
        tile = scale * lax.dot_general(
            images[:, :E], texts[cols, :], (((1,), (1,)), ((), ())), preferred_element_type=F32
        )
        logits[:, cols] = tile
        top = jnp.max(tile, axis=0, keepdims=True)
        total = jnp.sum(jnp.exp(tile - top), axis=0, keepdims=True)
        col_vec[:, cols] = top + jnp.log(total)

    pl.loop(0, 2)(logits_of)
    for q in range(2):
        for d in range(-3, 5):
            rows, i = theirs(q, d)
            arrived(texts.at[rows], sib_send.at[i], sib_recv.at[i], sibling)
    pl.loop(2, 4)(logits_of)
    send(col_vec, col_sib, stat_send, stat_recv, sibling)

    @pl.loop(0, 8)
    def _(n):
        rows = pl.ds(pl.multiple_of(n * 64, 64), 64)
        tile = logits[rows, :]
        top = jnp.max(tile, axis=1, keepdims=True)
        total = jnp.sum(jnp.exp(tile - top), axis=1, keepdims=True)
        row_stat[rows, :] = jnp.broadcast_to(top + jnp.log(total), (64, 128))

    row_ring[0] = jnp.transpose(row_stat[...])[0:1, :]

    for k in range(1, GROUP):
        send(row_ring.at[0], row_ring.at[k], srow_send.at[k], srow_recv.at[k], image_peers[k])
    arrived(col_sib, stat_send, stat_recv, sibling)
    from_sibling = col_sib[...]
    from_sibling = jnp.concatenate([from_sibling[:, HALF:], from_sibling[:, :HALF]], axis=1)
    col_ring[0] = lse2(col_vec[...], from_sibling)
    for k in range(1, GROUP):
        send(col_ring.at[0], col_ring.at[k], scol_send.at[k], scol_recv.at[k], text_peers[k])
    for k in range(1, GROUP):
        arrived(row_ring.at[k], srow_send.at[k], srow_recv.at[k], image_peers[k])

    def joined(ring):
        parts = [ring[k] for k in range(GROUP)]
        top = parts[0]
        for part in parts[1:]:
            top = jnp.maximum(top, part)
        total = jnp.exp(parts[0] - top)
        for part in parts[1:]:
            total = total + jnp.exp(part - top)
        return top + jnp.log(total)

    row_stat[...] = jnp.transpose(jnp.broadcast_to(joined(row_ring), (128, HALF)))
    for k in range(1, GROUP):
        arrived(col_ring.at[k], scol_send.at[k], scol_recv.at[k], text_peers[k])
    col_stat[...] = joined(col_ring)

    @pl.loop(0, 4)
    def _(n):
        rows = pl.ds(pl.multiple_of(n * 128, 128), 128)
        at_lane = lax.broadcasted_iota(jnp.int32, (1, 2 * HALF), 1)
        member = (at_lane >> 5) & 15
        its_y, parity = member >> 1, member & 1
        its_core = jnp.where(at_lane < HALF, core, 1 - core)
        its_x = jnp.where(parity == p, x, xb)
        its_blk = (its_x * 4 + (its_y & 3)) * 2 + its_core
        its_dp = (its_y >> 2) * 8 + z
        ids = ((its_blk * 16 + its_dp) * R + (at_lane & 31)).astype(F32)
        digit = images[rows, E:].astype(F32)
        label = digit[:, 0:1] * 128.0 + digit[:, 64:65]
        tile = logits[rows, :]
        target = jnp.where(label == ids, 2.0, 0.0)
        both = jnp.exp(tile - row_stat[rows, 0:1]) + jnp.exp(tile - col_stat[...])
        weight = (both - target) * 0.5
        wts[rows, :] = weight.astype(BF16)
        wts_t[:, rows] = jnp.transpose(weight).astype(BF16)

    for n in range(4):
        cols = pl.ds(n * 256, 256)
        swap_out[:, cols] = jnp.dot(
            wts_t[HALF:, :], images[:, cols], preferred_element_type=F32
        ).astype(BF16)
        send(swap_out.at[:, cols], swap_in.at[:, cols], swap_send.at[n], swap_recv.at[n], sibling)

    def summed(kind, piece):
        total = (grad_i if kind == 0 else grad_t)[piece_rows(kind, piece), :]
        for child in CHILDREN.get(piece, ()):
            i = index(kind, child)
            arrived(landed.at[i], rs_send.at[i], rs_recv.at[i], peer_of(kind, 0))
            total = total + landed[i].astype(F32)
        return total

    def pass_on(kind, piece):
        i = index(kind, piece)
        stage[i] = summed(kind, piece).astype(BF16)
        send(stage.at[i], landed.at[i], rs_send.at[i], rs_recv.at[i], peer_of(kind, -parent(piece)[1]))

    leaves = [piece for piece in BACKWARDS if piece not in CHILDREN]

    @pl.loop(0, 4)
    def _(n):
        cols = pl.ds(pl.multiple_of(n * 256, 256), 256)
        grad_i[:, cols] = jnp.dot(wts[...], texts[:, cols], preferred_element_type=F32)

    for piece in leaves:
        pass_on(0, piece)

    @pl.loop(0, 4)
    def _(n):
        cols = pl.ds(pl.multiple_of(n * 256, 256), 256)
        grad_t[:, cols] = jnp.dot(wts_t[:HALF, :], images[:, cols], preferred_element_type=F32)

    for n in range(4):
        cols = pl.ds(n * 256, 256)
        arrived(swap_in.at[:, cols], swap_send.at[n], swap_recv.at[n], sibling)
    grad_t[...] = grad_t[...] + swap_in[...].astype(F32)
    for piece in leaves:
        pass_on(1, piece)
    for piece in BACKWARDS:
        if piece in CHILDREN:
            for kind in range(2):
                pass_on(kind, piece)
    for kind, out_ref in ((0, out_image_ref), (1, out_text_ref)):
        for h in range(2):
            out_ref[pl.ds(h * H, H), :] = (scale * summed(kind, (0, h, 0))).astype(BF16)

    for one in sent:
        one.wait_send()


def per_device(image_emb, text_emb, labels, logit_scale):
    vmem = pl.BlockSpec(memory_space=pltpu.VMEM)
    smem = pl.BlockSpec(memory_space=pltpu.SMEM)
    hbm = pl.BlockSpec(memory_space=pltpu.HBM)
    dma = pltpu.SemaphoreType.DMA
    out = jax.ShapeDtypeStruct((R, E), BF16)
    return pl.pallas_call(
        kernel,
        out_shape=(out, out),
        in_specs=[hbm, hbm, hbm, smem],
        out_specs=(vmem, vmem),
        scratch_shapes=[
            pltpu.VMEM((HALF, W), BF16),
            pltpu.VMEM((2 * HALF, E), BF16),
            pltpu.VMEM((HALF, 2 * HALF), F32),
            pltpu.VMEM((HALF, 2 * HALF), BF16),
            pltpu.VMEM((2 * HALF, HALF), BF16),
            pltpu.VMEM((HALF, E), F32),
            pltpu.VMEM((HALF, E), F32),
            pltpu.VMEM((HALF, 128), F32),
            pltpu.VMEM((1, 2 * HALF), F32),
            pltpu.VMEM((GROUP, 1, HALF), F32),
            pltpu.VMEM((1, 2 * HALF), F32),
            pltpu.VMEM((1, 2 * HALF), F32),
            pltpu.VMEM((GROUP, 1, 2 * HALF), F32),
            pltpu.SMEM((R,), jnp.int32),
            pltpu.VMEM((HALF, E), BF16),
            pltpu.VMEM((HALF, E), BF16),
            pltpu.VMEM((2, 2, 2, RING, H, E), BF16),
            pltpu.VMEM((2, 2, 2, RING, H, E), BF16),
            dma((3,)),
            dma((2, 2, 2, RING)), dma((2, 2, 2, RING)),
            dma((2, RING)), dma((2, RING)),
            dma(()), dma(()),
            dma((GROUP,)), dma((GROUP,)),
            dma((GROUP,)), dma((GROUP,)),
            dma((4,)), dma((4,)),
            dma((2, 2, 2, RING)), dma((2, 2, 2, RING)),
        ],
        compiler_params=pltpu.CompilerParams(
            collective_id=0, has_side_effects=True, vmem_limit_bytes=40 * 1024 * 1024
        ),
        cost_estimate=pl.CostEstimate(flops=3221225472, bytes_accessed=262144, transcendentals=2097152),
        name="contrastive",
    )(image_emb, text_emb, labels, logit_scale.reshape(1))


def solution(mesh):
    in_specs = (P(("blk", "dp"), None), P(("blk", "dp"), None), P(("blk", "dp")), P())
    out_specs = (P(("blk", "dp"), None), P(("blk", "dp"), None))
    return jax.shard_map(
        per_device, mesh=mesh, in_specs=in_specs, out_specs=out_specs, check_vma=False
    )
```

```python
import jax
import jax.numpy as jnp
from jax import lax
from jax.experimental import pallas as pl
from jax.experimental.pallas import tpu as pltpu
from jax.sharding import PartitionSpec as P

R = 32
H = R // 2
E = 1024
RING = 8
HALF = RING * 2 * R
GROUP = 2 * RING
F32 = jnp.float32
BF16 = jnp.bfloat16
MESH = pl.DeviceIdType.MESH

STAGES = (
    ((1, 0, 0), (0, 1, 2), (0, 1, -2), (0, 0, 1), (0, 0, -1), (0, 1, 1), (0, 1, -1), (1, 1, 0)),
    (
        (1, 0, 2), (1, 0, -2), (0, 1, 4), (0, 1, 3), (0, 1, -3), (0, 0, 2), (0, 0, -2),
        (1, 0, 1), (1, 0, -1), (1, 1, 2), (1, 1, -2), (1, 1, 1), (1, 1, -1),
    ),
    (
        (0, 0, 4), (0, 0, 3), (0, 0, -3), (1, 0, 4), (1, 0, 3), (1, 0, -3),
        (1, 1, 4), (1, 1, 3), (1, 1, -3),
    ),
)


def parent(piece):
    q, h, d = piece
    if q == 1 and (h == 1 or d == 0):
        return (0, h, d), 0
    if d == 4:
        step = -2 if (q, h) == (0, 1) else 2
        return (q, h, step), step
    step = d if abs(d) == 2 and q != h else (1 if d > 0 else -1)
    return (q, h, d - step), step


CHILDREN = {}
for _stage in STAGES:
    for _piece in _stage:
        CHILDREN.setdefault(parent(_piece)[0], []).append(_piece)
BACKWARDS = [_piece for _stage in STAGES[::-1] for _piece in _stage]


def lse2(a, b):
    top = jnp.maximum(a, b)
    return top + jnp.log(jnp.exp(a - top) + jnp.exp(b - top))


def kernel(
    image_ref, text_ref, label_ref, scale_ref, out_image_ref, out_text_ref,
    images, texts, logits, wts, wts_t, grad_i, grad_t, row_stat, col_stat,
    row_ring, col_vec, col_sib, col_ring, label_stat, labels,
    swap_out, swap_in, grad_i16, grad_t16, stage, landed,
    load_sem, ring_send, ring_recv, sib_send, sib_recv, stat_send, stat_recv,
    srow_send, srow_recv, scol_send, scol_recv, swap_send, swap_recv, rs_send, rs_recv,
):
    blk, dp = lax.axis_index("blk"), lax.axis_index("dp")
    core, x = blk % 2, blk // 8
    y, z = (dp // 8) * 4 + (blk // 2) % 4, dp % 8
    p = x % 2
    xa = x + 1 - 2 * p
    xb = (x + 2 * p + 3) % 4
    sense = 1 - 2 * core

    def at(x=x, y=y, z=z, core=core):
        return {"blk": (x * 4 + y % 4) * 2 + core, "dp": (y // 4) * 8 + z}

    def along(v, d):
        return (v + sense * d + RING) % RING

    sibling = at(core=1 - core)
    image_peers = [at(x=x if q == 0 else xa, z=along(z, k)) for q in range(2) for k in range(RING)]
    text_peers = [at(x=x if q == 0 else xb, y=along(y, k)) for q in range(2) for k in range(RING)]

    own_image = pl.ds(pl.multiple_of((z * 2 + p) * R, R), R)
    own_text = pl.ds(pl.multiple_of((y * 2 + p) * R, R), R)
    loads = [
        pltpu.make_async_copy(label_ref, labels, load_sem.at[0]),
        pltpu.make_async_copy(image_ref, images.at[own_image], load_sem.at[1]),
        pltpu.make_async_copy(text_ref, texts.at[own_text], load_sem.at[2]),
    ]
    for load in loads:
        load.start()
    barrier = pltpu.get_barrier_semaphore()
    steps = (1, RING - 1, 2, RING - 2, RING)
    peers = [sibling] + [image_peers[k] for k in steps] + [text_peers[k] for k in steps]
    for peer in peers:
        pl.semaphore_signal(barrier, inc=1, device_id=peer, device_id_type=MESH)
    loads[1].wait()
    loads[2].wait()
    loads[0].wait()
    pl.semaphore_wait(barrier, len(peers))

    def copy(src, dst, ssem, rsem, peer):
        return pltpu.make_async_remote_copy(
            src_ref=src, dst_ref=dst, send_sem=ssem, recv_sem=rsem, device_id=peer, device_id_type=MESH
        )

    def send(src, dst, ssem, rsem, peer):
        copy(src, dst, ssem, rsem, peer).start()

    def arrived(dst, ssem, rsem):
        copy(dst, dst, ssem, rsem, sibling).wait_recv()

    def left(src, ssem, rsem):
        copy(src, src, ssem, rsem, sibling).wait_send()

    place = (z, y)

    def peer_of(kind, step):
        if step == 0:
            return at(x=xa) if kind == 0 else at(x=xb)
        return at(z=along(z, step)) if kind == 0 else at(y=along(y, step))

    def piece_rows(kind, piece):
        q, h, d = piece
        slot = along(place[kind], -d) * 2 + (p if q == 0 else 1 - p)
        return pl.ds(pl.multiple_of(slot * R + h * H, H), H)

    def held(kind, piece):
        return (images if kind == 0 else texts).at[piece_rows(kind, piece)]

    def index(kind, piece):
        q, h, d = piece
        return kind, q, h, d + 3

    def gather_send(kind, piece):
        source, step = parent(piece)
        part, i = held(kind, source), index(kind, piece)
        send(part, part, ring_send.at[kind], ring_recv.at[i], peer_of(kind, step))

    def to_sibling(d):
        slot = along(y, -d) * 2
        mine = pl.ds(pl.multiple_of(slot * R, 2 * R), 2 * R)
        there = pl.ds(pl.multiple_of(slot * R + HALF, 2 * R), 2 * R)
        send(texts.at[mine], texts.at[there], sib_send, sib_recv, sibling)

    for piece in STAGES[0]:
        for kind in range(2):
            gather_send(kind, piece)
    got = {(0, 0, 0), (0, 1, 0)}
    for pieces in STAGES:
        for piece in pieces:
            d = piece[2]
            for kind in (1, 0):
                i = index(kind, piece)
                arrived(held(kind, piece), ring_send.at[kind], ring_recv.at[i])
                for child in CHILDREN.get(piece, ()):
                    gather_send(kind, child)
                got.add(piece)
                if kind == 1 and all((q, h, d) in got for q in range(2) for h in range(2)):
                    to_sibling(d)

    scale = scale_ref[0]

    @pl.loop(0, 4)
    def _(n):
        @pl.when(n == 2)
        def _():
            arrived(texts.at[pl.ds(HALF, HALF)], sib_send, sib_recv)

        cols = pl.ds(pl.multiple_of(n * 256, 256), 256)
        tile = scale * lax.dot_general(
            images[...], texts[cols, :], (((1,), (1,)), ((), ())), preferred_element_type=F32
        )
        logits[:, cols] = tile
        top = jnp.max(tile, axis=0, keepdims=True)
        total = jnp.sum(jnp.exp(tile - top), axis=0, keepdims=True)
        col_vec[:, cols] = top + jnp.log(total)

    send(col_vec, col_sib, stat_send, stat_recv, sibling)

    at_label = lax.broadcasted_iota(jnp.int32, (1, HALF), 1) - (z * 2 + p) * R
    own_labels = jnp.zeros((1, HALF), jnp.int32)
    for r in range(R):
        own_labels = jnp.where(at_label == r, labels[r], own_labels)
    row_ring[0, 1:2, :] = own_labels.astype(F32)

    @pl.loop(0, 4)
    def _(n):
        @pl.when(n == 2)
        def _():
            arrived(col_sib, stat_send, stat_recv)
            from_sibling = col_sib[...]
            from_sibling = jnp.concatenate([from_sibling[:, HALF:], from_sibling[:, :HALF]], axis=1)
            col_ring[0] = lse2(col_vec[...], from_sibling)
            for k in range(1, GROUP):
                send(col_ring.at[0], col_ring.at[k], scol_send, scol_recv, text_peers[k])

        rows = pl.ds(pl.multiple_of(n * 128, 128), 128)
        tile = logits[rows, :]
        top = jnp.max(tile, axis=1, keepdims=True)
        total = jnp.sum(jnp.exp(tile - top), axis=1, keepdims=True)
        row_stat[rows, :] = jnp.broadcast_to(top + jnp.log(total), (128, 128))

    row_ring[0, 0:1, :] = jnp.transpose(row_stat[...])[0:1, :]
    for k in range(1, GROUP):
        send(row_ring.at[0], row_ring.at[k], srow_send, srow_recv, image_peers[k])

    gathered = pl.ds(0, HALF - R)
    left(images.at[gathered], ring_send.at[0], sib_recv)
    left(texts.at[gathered], ring_send.at[1], sib_recv)
    left(texts.at[pl.ds(0, HALF)], sib_send, sib_recv)
    left(col_vec, stat_send, stat_recv)

    def joined(ring):
        parts = [ring[k, 0:1, :] for k in range(GROUP)]
        top = parts[0]
        for part in parts[1:]:
            top = jnp.maximum(top, part)
        total = jnp.exp(parts[0] - top)
        for part in parts[1:]:
            total = total + jnp.exp(part - top)
        return top + jnp.log(total)

    others = pl.ds(1, GROUP - 1)
    arrived(col_ring.at[others], scol_send, scol_recv)
    col_stat[...] = joined(col_ring)
    arrived(row_ring.at[others], srow_send, srow_recv)
    row_stat[...] = jnp.transpose(jnp.broadcast_to(joined(row_ring), (128, HALF)))
    group_labels = row_ring[0, 1:2, :]
    for k in range(1, GROUP):
        group_labels = group_labels + row_ring[k, 1:2, :]
    label_stat[...] = jnp.transpose(jnp.broadcast_to(group_labels, (128, HALF)))
    left(col_ring.at[others], scol_send, scol_recv)
    left(row_ring.at[others], srow_send, srow_recv)

    @pl.loop(0, 4)
    def _(n):
        rows = pl.ds(pl.multiple_of(n * 128, 128), 128)
        at_lane = lax.broadcasted_iota(jnp.int32, (1, 2 * HALF), 1)
        member = (at_lane >> 5) & 15
        its_y, parity = member >> 1, member & 1
        its_core = jnp.where(at_lane < HALF, core, 1 - core)
        its_x = jnp.where(parity == p, x, xb)
        its_blk = (its_x * 4 + (its_y & 3)) * 2 + its_core
        its_dp = (its_y >> 2) * 8 + z
        ids = ((its_blk * 16 + its_dp) * R + (at_lane & 31)).astype(F32)
        tile = logits[rows, :]
        target = jnp.where(label_stat[rows, 0:1] == ids, 2.0, 0.0)
        both = jnp.exp(tile - row_stat[rows, 0:1]) + jnp.exp(tile - col_stat[...])
        weight = (both - target) * 0.5
        wts[rows, :] = weight.astype(BF16)
        wts_t[:, rows] = jnp.transpose(weight).astype(BF16)

    @pl.loop(0, 4)
    def _(n):
        cols = pl.ds(pl.multiple_of(n * 256, 256), 256)
        swap_out[:, cols] = jnp.dot(
            wts_t[HALF:, :], images[:, cols], preferred_element_type=F32
        ).astype(BF16)
        send(swap_out.at[:, cols], swap_in.at[:, cols], swap_send, swap_recv, sibling)

    def summed(kind, piece):
        total = (grad_i if kind == 0 else grad_t)[piece_rows(kind, piece), :]
        for child in CHILDREN.get(piece, ()):
            i = index(kind, child)
            arrived(landed.at[i], rs_send.at[kind], rs_recv.at[i])
            total = total + landed[i].astype(F32)
        return total

    def pass_on(kind, piece):
        i = index(kind, piece)
        if piece in CHILDREN:
            out = stage.at[i]
            out[...] = summed(kind, piece).astype(BF16)
        else:
            out = (grad_i16 if kind == 0 else grad_t16).at[piece_rows(kind, piece)]
        send(out, landed.at[i], rs_send.at[kind], rs_recv.at[i], peer_of(kind, -parent(piece)[1]))

    leaves = [piece for piece in BACKWARDS if piece not in CHILDREN]

    @pl.loop(0, 4)
    def _(n):
        cols = pl.ds(pl.multiple_of(n * 256, 256), 256)
        term = jnp.dot(wts[...], texts[:, cols], preferred_element_type=F32)
        grad_i[:, cols] = term
        grad_i16[:, cols] = term.astype(BF16)

    for piece in leaves:
        pass_on(0, piece)

    @pl.loop(0, 4)
    def _(n):
        cols = pl.ds(pl.multiple_of(n * 256, 256), 256)
        grad_t[:, cols] = jnp.dot(wts_t[:HALF, :], images[:, cols], preferred_element_type=F32)

    arrived(swap_in, swap_send, swap_recv)

    @pl.loop(0, 8)
    def _(n):
        rows = pl.ds(pl.multiple_of(n * 64, 64), 64)
        term = grad_t[rows, :] + swap_in[rows, :].astype(F32)
        grad_t[rows, :] = term
        grad_t16[rows, :] = term.astype(BF16)

    for piece in leaves:
        pass_on(1, piece)
    for piece in BACKWARDS:
        if piece in CHILDREN:
            for kind in range(2):
                pass_on(kind, piece)
    for kind, out_ref in ((0, out_image_ref), (1, out_text_ref)):
        for h in range(2):
            out_ref[pl.ds(h * H, H), :] = (scale * summed(kind, (0, h, 0))).astype(BF16)

    left(swap_out, swap_send, swap_recv)
    left(grad_i16.at[gathered], rs_send.at[0], swap_recv)
    left(grad_t16.at[gathered], rs_send.at[1], swap_recv)


def per_device(image_emb, text_emb, labels, logit_scale):
    vmem = pl.BlockSpec(memory_space=pltpu.VMEM)
    smem = pl.BlockSpec(memory_space=pltpu.SMEM)
    hbm = pl.BlockSpec(memory_space=pltpu.HBM)
    dma = pltpu.SemaphoreType.DMA
    out = jax.ShapeDtypeStruct((R, E), BF16)
    return pl.pallas_call(
        kernel,
        out_shape=(out, out),
        in_specs=[hbm, hbm, hbm, smem],
        out_specs=(vmem, vmem),
        scratch_shapes=[
            pltpu.VMEM((HALF, E), BF16),
            pltpu.VMEM((2 * HALF, E), BF16),
            pltpu.VMEM((HALF, 2 * HALF), F32),
            pltpu.VMEM((HALF, 2 * HALF), BF16),
            pltpu.VMEM((2 * HALF, HALF), BF16),
            pltpu.VMEM((HALF, E), F32),
            pltpu.VMEM((HALF, E), F32),
            pltpu.VMEM((HALF, 128), F32),
            pltpu.VMEM((1, 2 * HALF), F32),
            pltpu.VMEM((GROUP, 2, HALF), F32),
            pltpu.VMEM((1, 2 * HALF), F32),
            pltpu.VMEM((1, 2 * HALF), F32),
            pltpu.VMEM((GROUP, 1, 2 * HALF), F32),
            pltpu.VMEM((HALF, 128), F32),
            pltpu.SMEM((R,), jnp.int32),
            pltpu.VMEM((HALF, E), BF16),
            pltpu.VMEM((HALF, E), BF16),
            pltpu.VMEM((HALF, E), BF16),
            pltpu.VMEM((HALF, E), BF16),
            pltpu.VMEM((2, 2, 2, RING, H, E), BF16),
            pltpu.VMEM((2, 2, 2, RING, H, E), BF16),
            dma((3,)),
            dma((2,)), dma((2, 2, 2, RING)),
            dma(()), dma(()),
            dma(()), dma(()),
            dma(()), dma(()),
            dma(()), dma(()),
            dma(()), dma(()),
            dma((2,)), dma((2, 2, 2, RING)),
        ],
        compiler_params=pltpu.CompilerParams(
            collective_id=0, has_side_effects=True, vmem_limit_bytes=40 * 1024 * 1024
        ),
        cost_estimate=pl.CostEstimate(flops=3221225472, bytes_accessed=262144, transcendentals=2097152),
        name="contrastive",
    )(image_emb, text_emb, labels, logit_scale.reshape(1))


def solution(mesh):
    in_specs = (P(("blk", "dp"), None), P(("blk", "dp"), None), P(("blk", "dp")), P())
    out_specs = (P(("blk", "dp"), None), P(("blk", "dp"), None))
    return jax.shard_map(
        per_device, mesh=mesh, in_specs=in_specs, out_specs=out_specs, check_vma=False
    )
```

```python
import jax
import jax.numpy as jnp
from jax import lax
from jax.experimental import pallas as pl
from jax.experimental.pallas import tpu as pltpu
from jax.sharding import PartitionSpec as P

R = 32
H = R // 2
E = 1024
RING = 8
HALF = RING * 2 * R
GROUP = 2 * RING
F32 = jnp.float32
BF16 = jnp.bfloat16
MESH = pl.DeviceIdType.MESH

STAGES = (
    ((1, 0, 0), (0, 1, 2), (0, 1, -2), (0, 0, 1), (0, 0, -1), (0, 1, 1), (0, 1, -1), (1, 1, 0)),
    (
        (1, 0, 2), (1, 0, -2), (0, 1, 4), (0, 1, 3), (0, 1, -3), (0, 0, 2), (0, 0, -2),
        (1, 0, 1), (1, 0, -1), (1, 1, 2), (1, 1, -2), (1, 1, 1), (1, 1, -1),
    ),
    (
        (0, 0, 4), (0, 0, 3), (0, 0, -3), (1, 0, 4), (1, 0, 3), (1, 0, -3),
        (1, 1, 4), (1, 1, 3), (1, 1, -3),
    ),
)


def parent(piece):
    q, h, d = piece
    if q == 1 and (h == 1 or d == 0):
        return (0, h, d), 0
    if d == 4:
        step = -2 if (q, h) == (0, 1) else 2
        return (q, h, step), step
    step = d if abs(d) == 2 and q != h else (1 if d > 0 else -1)
    return (q, h, d - step), step


CHILDREN = {}
for _stage in STAGES:
    for _piece in _stage:
        CHILDREN.setdefault(parent(_piece)[0], []).append(_piece)
BACKWARDS = [_piece for _stage in STAGES[::-1] for _piece in _stage]


def lse2(a, b):
    top = jnp.maximum(a, b)
    return top + jnp.log(jnp.exp(a - top) + jnp.exp(b - top))


def kernel(
    image_ref, text_ref, label_ref, scale_ref, out_image_ref, out_text_ref,
    images, texts, logits, wts, wts_t, grad_i, grad_t, row_stat, col_stat,
    row_ring, col_vec, col_sib, col_ring, label_stat, labels,
    swap_out, swap_in, grad_i16, grad_t16, stage, landed,
    load_sem, ring_send, ring_recv, sib_send, sib_recv, stat_send, stat_recv,
    srow_send, srow_recv, scol_send, scol_recv, swap_send, swap_recv, rs_send, rs_recv,
):
    blk, dp = lax.axis_index("blk"), lax.axis_index("dp")
    core, x = blk % 2, blk // 8
    y, z = (dp // 8) * 4 + (blk // 2) % 4, dp % 8
    p = x % 2
    xa = x + 1 - 2 * p
    xb = (x + 2 * p + 3) % 4
    sense = 1 - 2 * core

    def at(x=x, y=y, z=z, core=core):
        return {"blk": (x * 4 + y % 4) * 2 + core, "dp": (y // 4) * 8 + z}

    def along(v, d):
        return (v + sense * d + RING) % RING

    sibling = at(core=1 - core)
    image_peers = [at(x=x if q == 0 else xa, z=along(z, k)) for q in range(2) for k in range(RING)]
    text_peers = [at(x=x if q == 0 else xb, y=along(y, k)) for q in range(2) for k in range(RING)]

    own_image = pl.ds(pl.multiple_of((z * 2 + p) * R, R), R)
    own_text = pl.ds(pl.multiple_of((y * 2 + p) * R, R), R)
    loads = [
        pltpu.make_async_copy(label_ref, labels, load_sem.at[0]),
        pltpu.make_async_copy(image_ref, images.at[own_image], load_sem.at[1]),
        pltpu.make_async_copy(text_ref, texts.at[own_text], load_sem.at[2]),
    ]
    for load in loads:
        load.start()
    barrier = pltpu.get_barrier_semaphore()
    steps = (1, RING - 1, 2, RING - 2, RING)
    peers = [sibling] + [image_peers[k] for k in steps] + [text_peers[k] for k in steps]
    for peer in peers:
        pl.semaphore_signal(barrier, inc=1, device_id=peer, device_id_type=MESH)
    loads[1].wait()
    loads[2].wait()
    loads[0].wait()
    pl.semaphore_wait(barrier, len(peers))

    def copy(src, dst, ssem, rsem, peer):
        return pltpu.make_async_remote_copy(
            src_ref=src, dst_ref=dst, send_sem=ssem, recv_sem=rsem, device_id=peer, device_id_type=MESH
        )

    def send(src, dst, ssem, rsem, peer):
        copy(src, dst, ssem, rsem, peer).start()

    def arrived(dst, ssem, rsem):
        copy(dst, dst, ssem, rsem, sibling).wait_recv()

    def left(src, ssem, rsem):
        copy(src, src, ssem, rsem, sibling).wait_send()

    place = (z, y)

    def peer_of(kind, step):
        if step == 0:
            return at(x=xa) if kind == 0 else at(x=xb)
        return at(z=along(z, step)) if kind == 0 else at(y=along(y, step))

    def piece_rows(kind, piece):
        q, h, d = piece
        slot = along(place[kind], -d) * 2 + (p if q == 0 else 1 - p)
        return pl.ds(pl.multiple_of(slot * R + h * H, H), H)

    def held(kind, piece):
        return (images if kind == 0 else texts).at[piece_rows(kind, piece)]

    def index(kind, piece):
        q, h, d = piece
        return kind, q, h, d + 3

    def gather_send(kind, piece):
        source, step = parent(piece)
        part, i = held(kind, source), index(kind, piece)
        send(part, part, ring_send.at[kind], ring_recv.at[i], peer_of(kind, step))

    def to_sibling(d):
        slot = along(y, -d) * 2
        mine = pl.ds(pl.multiple_of(slot * R, 2 * R), 2 * R)
        there = pl.ds(pl.multiple_of(slot * R + HALF, 2 * R), 2 * R)
        send(texts.at[mine], texts.at[there], sib_send, sib_recv, sibling)

    for piece in STAGES[0]:
        for kind in range(2):
            gather_send(kind, piece)
    got = {(0, 0, 0), (0, 1, 0)}
    for pieces in STAGES:
        for piece in pieces:
            d = piece[2]
            for kind in (1, 0):
                i = index(kind, piece)
                arrived(held(kind, piece), ring_send.at[kind], ring_recv.at[i])
                for child in CHILDREN.get(piece, ()):
                    gather_send(kind, child)
                got.add(piece)
                if kind == 1 and all((q, h, d) in got for q in range(2) for h in range(2)):
                    to_sibling(d)

    scale = scale_ref[0]

    @pl.loop(0, 4)
    def _(n):
        @pl.when(n == 2)
        def _():
            arrived(texts.at[pl.ds(HALF, HALF)], sib_send, sib_recv)

        cols = pl.ds(pl.multiple_of(n * 256, 256), 256)
        tile = scale * lax.dot_general(
            images[...], texts[cols, :], (((1,), (1,)), ((), ())), preferred_element_type=F32
        )
        logits[:, cols] = tile
        top = jnp.max(tile, axis=0, keepdims=True)
        total = jnp.sum(jnp.exp(tile - top), axis=0, keepdims=True)
        col_vec[:, cols] = top + jnp.log(total)

    send(col_vec, col_sib, stat_send, stat_recv, sibling)

    at_label = lax.broadcasted_iota(jnp.int32, (1, HALF), 1) - (z * 2 + p) * R
    own_labels = jnp.zeros((1, HALF), jnp.int32)
    for r in range(R):
        own_labels = jnp.where(at_label == r, labels[r], own_labels)
    row_ring[0, 1:2, :] = own_labels.astype(F32)

    @pl.loop(0, 2)
    def _(n):
        @pl.when(n == 1)
        def _():
            arrived(col_sib, stat_send, stat_recv)
            from_sibling = col_sib[...]
            from_sibling = jnp.concatenate([from_sibling[:, HALF:], from_sibling[:, :HALF]], axis=1)
            col_ring[0] = lse2(col_vec[...], from_sibling)
            for k in range(1, GROUP):
                send(col_ring.at[0], col_ring.at[k], scol_send, scol_recv, text_peers[k])

        rows = pl.ds(pl.multiple_of(n * 256, 256), 256)
        tile = logits[rows, :]
        top = jnp.max(tile, axis=1, keepdims=True)
        total = jnp.sum(jnp.exp(tile - top), axis=1, keepdims=True)
        row_stat[rows, :] = jnp.broadcast_to(top + jnp.log(total), (256, 128))

    row_ring[0, 0:1, :] = jnp.transpose(row_stat[...])[0:1, :]
    for k in range(1, GROUP):
        send(row_ring.at[0], row_ring.at[k], srow_send, srow_recv, image_peers[k])

    gathered = pl.ds(0, HALF - R)
    left(images.at[gathered], ring_send.at[0], sib_recv)
    left(texts.at[gathered], ring_send.at[1], sib_recv)
    left(texts.at[pl.ds(0, HALF)], sib_send, sib_recv)
    left(col_vec, stat_send, stat_recv)

    def joined(ring):
        parts = [ring[k, 0:1, :] for k in range(GROUP)]
        top = parts[0]
        for part in parts[1:]:
            top = jnp.maximum(top, part)
        total = jnp.exp(parts[0] - top)
        for part in parts[1:]:
            total = total + jnp.exp(part - top)
        return top + jnp.log(total)

    others = pl.ds(1, GROUP - 1)
    arrived(col_ring.at[others], scol_send, scol_recv)
    col_stat[...] = joined(col_ring)
    arrived(row_ring.at[others], srow_send, srow_recv)
    row_stat[...] = jnp.transpose(jnp.broadcast_to(joined(row_ring), (128, HALF)))
    group_labels = row_ring[0, 1:2, :]
    for k in range(1, GROUP):
        group_labels = group_labels + row_ring[k, 1:2, :]
    label_stat[...] = jnp.transpose(jnp.broadcast_to(group_labels, (128, HALF)))
    left(col_ring.at[others], scol_send, scol_recv)
    left(row_ring.at[others], srow_send, srow_recv)

    @pl.loop(0, 2)
    def _(n):
        rows = pl.ds(pl.multiple_of(n * 256, 256), 256)
        at_lane = lax.broadcasted_iota(jnp.int32, (1, 2 * HALF), 1)
        member = (at_lane >> 5) & 15
        its_y, parity = member >> 1, member & 1
        its_core = jnp.where(at_lane < HALF, core, 1 - core)
        its_x = jnp.where(parity == p, x, xb)
        its_blk = (its_x * 4 + (its_y & 3)) * 2 + its_core
        its_dp = (its_y >> 2) * 8 + z
        ids = ((its_blk * 16 + its_dp) * R + (at_lane & 31)).astype(F32)
        tile = logits[rows, :]
        target = jnp.where(label_stat[rows, 0:1] == ids, 2.0, 0.0)
        both = jnp.exp(tile - row_stat[rows, 0:1]) + jnp.exp(tile - col_stat[...])
        weight = (both - target) * 0.5
        wts[rows, :] = weight.astype(BF16)
        wts_t[:, rows] = jnp.transpose(weight).astype(BF16)

    def summed(kind, piece):
        total = (grad_i if kind == 0 else grad_t)[piece_rows(kind, piece), :]
        for child in CHILDREN.get(piece, ()):
            i = index(kind, child)
            arrived(landed.at[i], rs_send.at[kind], rs_recv.at[i])
            total = total + landed[i].astype(F32)
        return total

    def pass_on(kind, piece):
        i = index(kind, piece)
        if piece in CHILDREN:
            out = stage.at[i]
            out[...] = summed(kind, piece).astype(BF16)
        else:
            out = (grad_i16 if kind == 0 else grad_t16).at[piece_rows(kind, piece)]
        send(out, landed.at[i], rs_send.at[kind], rs_recv.at[i], peer_of(kind, -parent(piece)[1]))

    def band(kind, d, start=0):
        return pl.ds(pl.multiple_of(along(place[kind], -d) * 2 * R + start, 2 * R), 2 * R)

    def parts(term, bands):
        return [(d, term[n * 2 * R : (n + 1) * 2 * R, :]) for n, d in enumerate(bands)]

    def sibling_bands(bands):
        left_side = jnp.concatenate([wts_t[band(1, d, HALF), :] for d in bands], axis=0)
        term = jnp.dot(left_side, images[...], preferred_element_type=F32)
        for d, part in parts(term, bands):
            rows = band(1, d)
            swap_out[rows, :] = part.astype(BF16)
            theirs = swap_recv.at[(d if d == 4 else -d) + 3]
            send(swap_out.at[rows], swap_in.at[rows], swap_send, theirs, sibling)

    def image_bands(bands):
        left_side = jnp.concatenate([wts[band(0, d), :] for d in bands], axis=0)
        term = jnp.dot(left_side, texts[...], preferred_element_type=F32)
        for d, part in parts(term, bands):
            grad_i[band(0, d), :] = part
            grad_i16[band(0, d), :] = part.astype(BF16)

    def text_bands(bands):
        left_side = jnp.concatenate([wts_t[band(1, d), :] for d in bands], axis=0)
        term = jnp.dot(left_side, images[...], preferred_element_type=F32)
        for d, part in parts(term, bands):
            rows = band(1, d)
            arrived(swap_in.at[rows], swap_send, swap_recv.at[d + 3])
            total = part + swap_in[rows, :].astype(F32)
            grad_t[rows, :] = total
            grad_t16[rows, :] = total.astype(BF16)

    for bands in ((4, 3, -3), (2, -2, 1, -1, 0)):
        leaves = [piece for piece in BACKWARDS if piece not in CHILDREN and piece[2] in bands]
        sibling_bands(bands)
        image_bands(bands)
        for piece in leaves:
            pass_on(0, piece)
        text_bands(bands)
        for piece in leaves:
            pass_on(1, piece)
    for piece in BACKWARDS:
        if piece in CHILDREN:
            for kind in range(2):
                pass_on(kind, piece)
    for kind, out_ref in ((0, out_image_ref), (1, out_text_ref)):
        for h in range(2):
            out_ref[pl.ds(h * H, H), :] = (scale * summed(kind, (0, h, 0))).astype(BF16)

    left(swap_out, swap_send, swap_recv.at[0])
    left(grad_i16.at[gathered], rs_send.at[0], swap_recv.at[0])
    left(grad_t16.at[gathered], rs_send.at[1], swap_recv.at[0])


def per_device(image_emb, text_emb, labels, logit_scale):
    vmem = pl.BlockSpec(memory_space=pltpu.VMEM)
    smem = pl.BlockSpec(memory_space=pltpu.SMEM)
    hbm = pl.BlockSpec(memory_space=pltpu.HBM)
    dma = pltpu.SemaphoreType.DMA
    out = jax.ShapeDtypeStruct((R, E), BF16)
    return pl.pallas_call(
        kernel,
        out_shape=(out, out),
        in_specs=[hbm, hbm, hbm, smem],
        out_specs=(vmem, vmem),
        scratch_shapes=[
            pltpu.VMEM((HALF, E), BF16),
            pltpu.VMEM((2 * HALF, E), BF16),
            pltpu.VMEM((HALF, 2 * HALF), F32),
            pltpu.VMEM((HALF, 2 * HALF), BF16),
            pltpu.VMEM((2 * HALF, HALF), BF16),
            pltpu.VMEM((HALF, E), F32),
            pltpu.VMEM((HALF, E), F32),
            pltpu.VMEM((HALF, 128), F32),
            pltpu.VMEM((1, 2 * HALF), F32),
            pltpu.VMEM((GROUP, 2, HALF), F32),
            pltpu.VMEM((1, 2 * HALF), F32),
            pltpu.VMEM((1, 2 * HALF), F32),
            pltpu.VMEM((GROUP, 1, 2 * HALF), F32),
            pltpu.VMEM((HALF, 128), F32),
            pltpu.SMEM((R,), jnp.int32),
            pltpu.VMEM((HALF, E), BF16),
            pltpu.VMEM((HALF, E), BF16),
            pltpu.VMEM((HALF, E), BF16),
            pltpu.VMEM((HALF, E), BF16),
            pltpu.VMEM((2, 2, 2, RING, H, E), BF16),
            pltpu.VMEM((2, 2, 2, RING, H, E), BF16),
            dma((3,)),
            dma((2,)), dma((2, 2, 2, RING)),
            dma(()), dma(()),
            dma(()), dma(()),
            dma(()), dma(()),
            dma(()), dma(()),
            dma(()), dma((RING,)),
            dma((2,)), dma((2, 2, 2, RING)),
        ],
        compiler_params=pltpu.CompilerParams(
            collective_id=0, has_side_effects=True, vmem_limit_bytes=40 * 1024 * 1024
        ),
        cost_estimate=pl.CostEstimate(flops=3221225472, bytes_accessed=262144, transcendentals=2097152),
        name="contrastive",
    )(image_emb, text_emb, labels, logit_scale.reshape(1))


def solution(mesh):
    in_specs = (P(("blk", "dp"), None), P(("blk", "dp"), None), P(("blk", "dp")), P())
    out_specs = (P(("blk", "dp"), None), P(("blk", "dp"), None))
    return jax.shard_map(
        per_device, mesh=mesh, in_specs=in_specs, out_specs=out_specs, check_vma=False
    )
```

```python
import jax
import jax.numpy as jnp
from jax import lax
from jax.experimental import pallas as pl
from jax.experimental.pallas import tpu as pltpu
from jax.sharding import PartitionSpec as P

R = 32
H = R // 2
E = 1024
RING = 8
HALF = RING * 2 * R
GROUP = 2 * RING
F32 = jnp.float32
BF16 = jnp.bfloat16
MESH = pl.DeviceIdType.MESH

STAGES = (
    ((1, 0, 0), (0, 1, 2), (0, 1, -2), (0, 0, 1), (0, 0, -1), (0, 1, 1), (0, 1, -1), (1, 1, 0)),
    (
        (1, 0, 2), (1, 0, -2), (0, 1, 4), (0, 1, 3), (0, 1, -3), (0, 0, 2), (0, 0, -2),
        (1, 0, 1), (1, 0, -1), (1, 1, 2), (1, 1, -2), (1, 1, 1), (1, 1, -1),
    ),
    (
        (0, 0, 4), (0, 0, 3), (0, 0, -3), (1, 0, 4), (1, 0, 3), (1, 0, -3),
        (1, 1, 4), (1, 1, 3), (1, 1, -3),
    ),
)


def parent(piece):
    q, h, d = piece
    if q == 1 and (h == 1 or d == 0):
        return (0, h, d), 0
    if d == 4:
        step = -2 if (q, h) == (0, 1) else 2
        return (q, h, step), step
    step = d if abs(d) == 2 and q != h else (1 if d > 0 else -1)
    return (q, h, d - step), step


CHILDREN = {}
for _stage in STAGES:
    for _piece in _stage:
        CHILDREN.setdefault(parent(_piece)[0], []).append(_piece)
BACKWARDS = [_piece for _stage in STAGES[::-1] for _piece in _stage]


def lse2(a, b):
    top = jnp.maximum(a, b)
    return top + jnp.log(jnp.exp(a - top) + jnp.exp(b - top))


def kernel(
    image_ref, text_ref, label_ref, scale_ref, out_image_ref, out_text_ref,
    images, texts, logits, wts, wts_t, grad_i, grad_t, row_stat, col_stat,
    row_ring, col_vec, col_sib, col_ring, label_stat, labels,
    swap_out, swap_in, grad_i16, grad_t16, stage, landed,
    load_sem, ring_send, ring_recv, sib_send, sib_recv, stat_send, stat_recv,
    srow_send, srow_recv, scol_send, scol_recv, swap_send, swap_recv, rs_send, rs_recv,
):
    blk, dp = lax.axis_index("blk"), lax.axis_index("dp")
    core, x = blk % 2, blk // 8
    y, z = (dp // 8) * 4 + (blk // 2) % 4, dp % 8
    p = x % 2
    xa = x + 1 - 2 * p
    xb = (x + 2 * p + 3) % 4
    sense = 1 - 2 * core

    def at(x=x, y=y, z=z, core=core):
        return {"blk": (x * 4 + y % 4) * 2 + core, "dp": (y // 4) * 8 + z}

    def along(v, d):
        return (v + sense * d + RING) % RING

    sibling = at(core=1 - core)
    image_peers = [at(x=x if q == 0 else xa, z=along(z, k)) for q in range(2) for k in range(RING)]
    text_peers = [at(x=x if q == 0 else xb, y=along(y, k)) for q in range(2) for k in range(RING)]

    own_image = pl.ds(pl.multiple_of((z * 2 + p) * R, R), R)
    own_text = pl.ds(pl.multiple_of((y * 2 + p) * R, R), R)
    loads = [
        pltpu.make_async_copy(label_ref, labels, load_sem.at[0]),
        pltpu.make_async_copy(image_ref, images.at[own_image], load_sem.at[1]),
        pltpu.make_async_copy(text_ref, texts.at[own_text], load_sem.at[2]),
    ]
    for load in loads:
        load.start()
    barrier = pltpu.get_barrier_semaphore()
    steps = (1, RING - 1, 2, RING - 2, RING)
    peers = [sibling] + [image_peers[k] for k in steps] + [text_peers[k] for k in steps]
    for peer in peers:
        pl.semaphore_signal(barrier, inc=1, device_id=peer, device_id_type=MESH)
    loads[1].wait()
    loads[2].wait()
    loads[0].wait()
    pl.semaphore_wait(barrier, len(peers))

    def copy(src, dst, ssem, rsem, peer):
        return pltpu.make_async_remote_copy(
            src_ref=src, dst_ref=dst, send_sem=ssem, recv_sem=rsem, device_id=peer, device_id_type=MESH
        )

    def send(src, dst, ssem, rsem, peer):
        copy(src, dst, ssem, rsem, peer).start()

    def arrived(dst, ssem, rsem):
        copy(dst, dst, ssem, rsem, sibling).wait_recv()

    def left(src, ssem, rsem):
        copy(src, src, ssem, rsem, sibling).wait_send()

    place = (z, y)

    def peer_of(kind, step):
        if step == 0:
            return at(x=xa) if kind == 0 else at(x=xb)
        return at(z=along(z, step)) if kind == 0 else at(y=along(y, step))

    def piece_rows(kind, piece):
        q, h, d = piece
        slot = along(place[kind], -d) * 2 + (p if q == 0 else 1 - p)
        return pl.ds(pl.multiple_of(slot * R + h * H, H), H)

    def held(kind, piece):
        return (images if kind == 0 else texts).at[piece_rows(kind, piece)]

    def index(kind, piece):
        q, h, d = piece
        return kind, q, h, d + 3

    def gather_send(kind, piece):
        source, step = parent(piece)
        part, i = held(kind, source), index(kind, piece)
        send(part, part, ring_send.at[kind], ring_recv.at[i], peer_of(kind, step))

    def to_sibling(d):
        slot = along(y, -d) * 2
        mine = pl.ds(pl.multiple_of(slot * R, 2 * R), 2 * R)
        there = pl.ds(pl.multiple_of(slot * R + HALF, 2 * R), 2 * R)
        send(texts.at[mine], texts.at[there], sib_send, sib_recv, sibling)

    for piece in STAGES[0]:
        for kind in range(2):
            gather_send(kind, piece)
    at_label = lax.broadcasted_iota(jnp.int32, (1, HALF), 1) - (z * 2 + p) * R
    own_labels = jnp.zeros((1, HALF), jnp.int32)
    for r in range(R):
        own_labels = jnp.where(at_label == r, labels[r], own_labels)
    row_ring[0, 1:2, :] = own_labels.astype(F32)

    got = {(0, 0, 0), (0, 1, 0)}
    for pieces in STAGES:
        for piece in pieces:
            d = piece[2]
            for kind in (1, 0):
                i = index(kind, piece)
                arrived(held(kind, piece), ring_send.at[kind], ring_recv.at[i])
                for child in CHILDREN.get(piece, ()):
                    gather_send(kind, child)
                got.add(piece)
                if kind == 1 and all((q, h, d) in got for q in range(2) for h in range(2)):
                    to_sibling(d)

    scale = scale_ref[0]

    @pl.loop(0, 4)
    def _(n):
        @pl.when(n == 2)
        def _():
            arrived(texts.at[pl.ds(HALF, HALF)], sib_send, sib_recv)

        cols = pl.ds(pl.multiple_of(n * 256, 256), 256)
        tile = scale * lax.dot_general(
            images[...], texts[cols, :], (((1,), (1,)), ((), ())), preferred_element_type=F32
        )
        logits[:, cols] = tile
        top = jnp.max(tile, axis=0, keepdims=True)
        total = jnp.sum(jnp.exp(tile - top), axis=0, keepdims=True)
        col_vec[:, cols] = top + jnp.log(total)

    send(col_vec, col_sib, stat_send, stat_recv, sibling)

    @pl.loop(0, 2)
    def _(n):
        @pl.when(n == 1)
        def _():
            arrived(col_sib, stat_send, stat_recv)
            from_sibling = col_sib[...]
            from_sibling = jnp.concatenate([from_sibling[:, HALF:], from_sibling[:, :HALF]], axis=1)
            col_ring[0] = lse2(col_vec[...], from_sibling)
            for k in range(1, GROUP):
                send(col_ring.at[0], col_ring.at[k], scol_send, scol_recv, text_peers[k])

        rows = pl.ds(pl.multiple_of(n * 256, 256), 256)
        tile = logits[rows, :]
        top = jnp.max(tile, axis=1, keepdims=True)
        total = jnp.sum(jnp.exp(tile - top), axis=1, keepdims=True)
        row_stat[rows, :] = jnp.broadcast_to(top + jnp.log(total), (256, 128))

    row_ring[0, 0:1, :] = jnp.transpose(row_stat[...])[0:1, :]
    for k in range(1, GROUP):
        send(row_ring.at[0], row_ring.at[k], srow_send, srow_recv, image_peers[k])

    gathered = pl.ds(0, HALF - R)
    left(images.at[gathered], ring_send.at[0], sib_recv)
    left(texts.at[gathered], ring_send.at[1], sib_recv)
    left(texts.at[pl.ds(0, HALF)], sib_send, sib_recv)
    left(col_vec, stat_send, stat_recv)

    def joined(ring):
        parts = [ring[k, 0:1, :] for k in range(GROUP)]
        top = parts[0]
        for part in parts[1:]:
            top = jnp.maximum(top, part)
        total = jnp.exp(parts[0] - top)
        for part in parts[1:]:
            total = total + jnp.exp(part - top)
        return top + jnp.log(total)

    others = pl.ds(1, GROUP - 1)
    arrived(col_ring.at[others], scol_send, scol_recv)
    col_stat[...] = joined(col_ring)
    arrived(row_ring.at[others], srow_send, srow_recv)
    row_stat[...] = jnp.transpose(jnp.broadcast_to(joined(row_ring), (128, HALF)))
    group_labels = row_ring[0, 1:2, :]
    for k in range(1, GROUP):
        group_labels = group_labels + row_ring[k, 1:2, :]
    label_stat[...] = jnp.transpose(jnp.broadcast_to(group_labels, (128, HALF)))
    left(col_ring.at[others], scol_send, scol_recv)
    left(row_ring.at[others], srow_send, srow_recv)

    @pl.loop(0, 1)
    def _(n):
        rows = pl.ds(pl.multiple_of(n * 512, 512), 512)
        at_lane = lax.broadcasted_iota(jnp.int32, (1, 2 * HALF), 1)
        member = (at_lane >> 5) & 15
        its_y, parity = member >> 1, member & 1
        its_core = jnp.where(at_lane < HALF, core, 1 - core)
        its_x = jnp.where(parity == p, x, xb)
        its_blk = (its_x * 4 + (its_y & 3)) * 2 + its_core
        its_dp = (its_y >> 2) * 8 + z
        ids = ((its_blk * 16 + its_dp) * R + (at_lane & 31)).astype(F32)
        tile = logits[rows, :]
        target = jnp.where(label_stat[rows, 0:1] == ids, 2.0, 0.0)
        both = jnp.exp(tile - row_stat[rows, 0:1]) + jnp.exp(tile - col_stat[...])
        weight = (both - target) * 0.5
        wts[rows, :] = weight.astype(BF16)
        wts_t[:, rows] = jnp.transpose(weight).astype(BF16)

    def summed(kind, piece):
        total = (grad_i if kind == 0 else grad_t)[piece_rows(kind, piece), :]
        for child in CHILDREN.get(piece, ()):
            i = index(kind, child)
            arrived(landed.at[i], rs_send.at[kind], rs_recv.at[i])
            total = total + landed[i].astype(F32)
        return total

    def pass_on(kind, piece):
        i = index(kind, piece)
        if piece in CHILDREN:
            out = stage.at[i]
            out[...] = summed(kind, piece).astype(BF16)
        else:
            out = (grad_i16 if kind == 0 else grad_t16).at[piece_rows(kind, piece)]
        send(out, landed.at[i], rs_send.at[kind], rs_recv.at[i], peer_of(kind, -parent(piece)[1]))

    def band(kind, d, start=0):
        return pl.ds(pl.multiple_of(along(place[kind], -d) * 2 * R + start, 2 * R), 2 * R)

    def parts(term, bands):
        return [(d, term[n * 2 * R : (n + 1) * 2 * R, :]) for n, d in enumerate(bands)]

    def sibling_bands(bands):
        left_side = jnp.concatenate([wts_t[band(1, d, HALF), :] for d in bands], axis=0)
        term = jnp.dot(left_side, images[...], preferred_element_type=F32)
        for d, part in parts(term, bands):
            rows = band(1, d)
            swap_out[rows, :] = part.astype(BF16)
            theirs = swap_recv.at[(d if d == 4 else -d) + 3]
            send(swap_out.at[rows], swap_in.at[rows], swap_send, theirs, sibling)

    def image_bands(bands):
        left_side = jnp.concatenate([wts[band(0, d), :] for d in bands], axis=0)
        term = jnp.dot(left_side, texts[...], preferred_element_type=F32)
        for d, part in parts(term, bands):
            grad_i[band(0, d), :] = part
            grad_i16[band(0, d), :] = part.astype(BF16)

    def text_bands(bands):
        left_side = jnp.concatenate([wts_t[band(1, d), :] for d in bands], axis=0)
        term = jnp.dot(left_side, images[...], preferred_element_type=F32)
        for d, part in parts(term, bands):
            rows = band(1, d)
            arrived(swap_in.at[rows], swap_send, swap_recv.at[d + 3])
            total = part + swap_in[rows, :].astype(F32)
            grad_t[rows, :] = total
            grad_t16[rows, :] = total.astype(BF16)

    for bands in ((4, 3, -3), (2, -2, 1, -1, 0)):
        leaves = [piece for piece in BACKWARDS if piece not in CHILDREN and piece[2] in bands]
        sibling_bands(bands)
        image_bands(bands)
        for piece in leaves:
            pass_on(0, piece)
        text_bands(bands)
        for piece in leaves:
            pass_on(1, piece)
    for piece in BACKWARDS:
        if piece in CHILDREN:
            for kind in range(2):
                pass_on(kind, piece)
    for kind, out_ref in ((0, out_image_ref), (1, out_text_ref)):
        for h in range(2):
            out_ref[pl.ds(h * H, H), :] = scale * summed(kind, (0, h, 0))

    left(swap_out, swap_send, swap_recv.at[0])
    left(grad_i16.at[gathered], rs_send.at[0], swap_recv.at[0])
    left(grad_t16.at[gathered], rs_send.at[1], swap_recv.at[0])


def per_device(image_emb, text_emb, labels, logit_scale):
    vmem = pl.BlockSpec(memory_space=pltpu.VMEM)
    smem = pl.BlockSpec(memory_space=pltpu.SMEM)
    hbm = pl.BlockSpec(memory_space=pltpu.HBM)
    dma = pltpu.SemaphoreType.DMA
    out = jax.ShapeDtypeStruct((R, E), F32)
    grads = pl.pallas_call(
        kernel,
        out_shape=(out, out),
        in_specs=[hbm, hbm, hbm, smem],
        out_specs=(vmem, vmem),
        scratch_shapes=[
            pltpu.VMEM((HALF, E), BF16),
            pltpu.VMEM((2 * HALF, E), BF16),
            pltpu.VMEM((HALF, 2 * HALF), F32),
            pltpu.VMEM((HALF, 2 * HALF), BF16),
            pltpu.VMEM((2 * HALF, HALF), BF16),
            pltpu.VMEM((HALF, E), F32),
            pltpu.VMEM((HALF, E), F32),
            pltpu.VMEM((HALF, 128), F32),
            pltpu.VMEM((1, 2 * HALF), F32),
            pltpu.VMEM((GROUP, 2, HALF), F32),
            pltpu.VMEM((1, 2 * HALF), F32),
            pltpu.VMEM((1, 2 * HALF), F32),
            pltpu.VMEM((GROUP, 1, 2 * HALF), F32),
            pltpu.VMEM((HALF, 128), F32),
            pltpu.SMEM((R,), jnp.int32),
            pltpu.VMEM((HALF, E), BF16),
            pltpu.VMEM((HALF, E), BF16),
            pltpu.VMEM((HALF, E), BF16),
            pltpu.VMEM((HALF, E), BF16),
            pltpu.VMEM((2, 2, 2, RING, H, E), BF16),
            pltpu.VMEM((2, 2, 2, RING, H, E), BF16),
            dma((3,)),
            dma((2,)), dma((2, 2, 2, RING)),
            dma(()), dma(()),
            dma(()), dma(()),
            dma(()), dma(()),
            dma(()), dma(()),
            dma(()), dma((RING,)),
            dma((2,)), dma((2, 2, 2, RING)),
        ],
        compiler_params=pltpu.CompilerParams(
            collective_id=0, has_side_effects=True, vmem_limit_bytes=56 * 1024 * 1024
        ),
        cost_estimate=pl.CostEstimate(flops=3221225472, bytes_accessed=262144, transcendentals=2097152),
        name="contrastive",
    )(image_emb, text_emb, labels, logit_scale.reshape(1))
    return tuple(grad.astype(BF16) for grad in grads)


def solution(mesh):
    in_specs = (P(("blk", "dp"), None), P(("blk", "dp"), None), P(("blk", "dp")), P())
    out_specs = (P(("blk", "dp"), None), P(("blk", "dp"), None))
    return jax.shard_map(
        per_device, mesh=mesh, in_specs=in_specs, out_specs=out_specs, check_vma=False
    )
```

```python
import jax
import jax.numpy as jnp
from jax import lax
from jax.experimental import pallas as pl
from jax.experimental.pallas import tpu as pltpu
from jax.sharding import PartitionSpec as P

R = 32
H = R // 2
E = 1024
RING = 8
HALF = RING * 2 * R
GROUP = 2 * RING
F32 = jnp.float32
BF16 = jnp.bfloat16
MESH = pl.DeviceIdType.MESH

STAGES = (
    ((1, 0, 0), (0, 1, 2), (0, 1, -2), (0, 0, 1), (0, 0, -1), (0, 1, 1), (0, 1, -1), (1, 1, 0)),
    (
        (1, 0, 2), (1, 0, -2), (0, 1, 4), (0, 1, 3), (0, 1, -3), (0, 0, 2), (0, 0, -2),
        (1, 0, 1), (1, 0, -1), (1, 1, 2), (1, 1, -2), (1, 1, 1), (1, 1, -1),
    ),
    (
        (0, 0, 4), (0, 0, 3), (0, 0, -3), (1, 0, 4), (1, 0, 3), (1, 0, -3),
        (1, 1, 4), (1, 1, 3), (1, 1, -3),
    ),
)


def parent(piece):
    q, h, d = piece
    if q == 1 and (h == 1 or abs(d) < 2):
        return (0, h, d), 0
    if d == 4:
        step = -2 if (q, h) == (0, 1) else 2
        return (q, h, step), step
    step = d if abs(d) == 2 and q != h else (1 if d > 0 else -1)
    return (q, h, d - step), step


CHILDREN = {}
for _stage in STAGES:
    for _piece in _stage:
        CHILDREN.setdefault(parent(_piece)[0], []).append(_piece)
BACKWARDS = [_piece for _stage in STAGES[::-1] for _piece in _stage]


def lse2(a, b):
    top = jnp.maximum(a, b)
    return top + jnp.log(jnp.exp(a - top) + jnp.exp(b - top))


def kernel(
    image_ref, text_ref, label_ref, scale_ref, out_image_ref, out_text_ref,
    images, texts, logits, wts, wts_t, grad_i, grad_t, row_stat, col_stat,
    row_ring, col_vec, col_sib, col_ring, label_stat, labels,
    swap_out, swap_in, grad_i16, grad_t16, stage, landed,
    load_sem, ring_send, ring_recv, sib_send, sib_recv, stat_send, stat_recv,
    srow_send, srow_recv, scol_send, scol_recv, swap_send, swap_recv, rs_send, rs_recv,
):
    blk, dp = lax.axis_index("blk"), lax.axis_index("dp")
    core, x = blk % 2, blk // 8
    y, z = (dp // 8) * 4 + (blk // 2) % 4, dp % 8
    p = x % 2
    xa = x + 1 - 2 * p
    xb = (x + 2 * p + 3) % 4
    sense = 1 - 2 * core

    def at(x=x, y=y, z=z, core=core):
        return {"blk": (x * 4 + y % 4) * 2 + core, "dp": (y // 4) * 8 + z}

    def along(v, d):
        return (v + sense * d + RING) % RING

    sibling = at(core=1 - core)
    image_peers = [at(x=x if q == 0 else xa, z=along(z, k)) for q in range(2) for k in range(RING)]
    text_peers = [at(x=x if q == 0 else xb, y=along(y, k)) for q in range(2) for k in range(RING)]

    own_image = pl.ds(pl.multiple_of((z * 2 + p) * R, R), R)
    own_text = pl.ds(pl.multiple_of((y * 2 + p) * R, R), R)
    loads = [
        pltpu.make_async_copy(label_ref, labels, load_sem.at[0]),
        pltpu.make_async_copy(image_ref, images.at[own_image], load_sem.at[1]),
        pltpu.make_async_copy(text_ref, texts.at[own_text], load_sem.at[2]),
    ]
    for load in loads:
        load.start()
    barrier = pltpu.get_barrier_semaphore()
    steps = (1, RING - 1, 2, RING - 2, RING)
    peers = [sibling] + [image_peers[k] for k in steps] + [text_peers[k] for k in steps]
    for peer in peers:
        pl.semaphore_signal(barrier, inc=1, device_id=peer, device_id_type=MESH)
    loads[1].wait()
    loads[2].wait()
    loads[0].wait()
    pl.semaphore_wait(barrier, len(peers))

    def copy(src, dst, ssem, rsem, peer):
        return pltpu.make_async_remote_copy(
            src_ref=src, dst_ref=dst, send_sem=ssem, recv_sem=rsem, device_id=peer, device_id_type=MESH
        )

    def send(src, dst, ssem, rsem, peer):
        copy(src, dst, ssem, rsem, peer).start()

    def arrived(dst, ssem, rsem):
        copy(dst, dst, ssem, rsem, sibling).wait_recv()

    def left(src, ssem, rsem):
        copy(src, src, ssem, rsem, sibling).wait_send()

    place = (z, y)

    def peer_of(kind, step):
        if step == 0:
            return at(x=xa) if kind == 0 else at(x=xb)
        return at(z=along(z, step)) if kind == 0 else at(y=along(y, step))

    def piece_rows(kind, piece):
        q, h, d = piece
        slot = along(place[kind], -d) * 2 + (p if q == 0 else 1 - p)
        return pl.ds(pl.multiple_of(slot * R + h * H, H), H)

    def held(kind, piece):
        return (images if kind == 0 else texts).at[piece_rows(kind, piece)]

    def index(kind, piece):
        q, h, d = piece
        return kind, q, h, d + 3

    def gather_send(kind, piece):
        source, step = parent(piece)
        part, i = held(kind, source), index(kind, piece)
        send(part, part, ring_send.at[kind], ring_recv.at[i], peer_of(kind, step))

    def to_sibling(d):
        slot = along(y, -d) * 2
        mine = pl.ds(pl.multiple_of(slot * R, 2 * R), 2 * R)
        there = pl.ds(pl.multiple_of(slot * R + HALF, 2 * R), 2 * R)
        send(texts.at[mine], texts.at[there], sib_send, sib_recv, sibling)

    for piece in STAGES[0]:
        for kind in range(2):
            gather_send(kind, piece)
    at_label = lax.broadcasted_iota(jnp.int32, (1, HALF), 1) - (z * 2 + p) * R
    own_labels = jnp.zeros((1, HALF), jnp.int32)
    for r in range(R):
        own_labels = jnp.where(at_label == r, labels[r], own_labels)
    row_ring[0, 1:2, :] = own_labels.astype(F32)

    got = {(0, 0, 0), (0, 1, 0)}
    for pieces in STAGES:
        for piece in pieces:
            d = piece[2]
            for kind in (1, 0):
                i = index(kind, piece)
                arrived(held(kind, piece), ring_send.at[kind], ring_recv.at[i])
                for child in CHILDREN.get(piece, ()):
                    gather_send(kind, child)
                got.add(piece)
                if kind == 1 and all((q, h, d) in got for q in range(2) for h in range(2)):
                    to_sibling(d)

    scale = scale_ref[0]

    @pl.loop(0, 4)
    def _(n):
        @pl.when(n == 2)
        def _():
            arrived(texts.at[pl.ds(HALF, HALF)], sib_send, sib_recv)

        cols = pl.ds(pl.multiple_of(n * 256, 256), 256)
        tile = scale * lax.dot_general(
            images[...], texts[cols, :], (((1,), (1,)), ((), ())), preferred_element_type=F32
        )
        logits[:, cols] = tile
        top = jnp.max(tile, axis=0, keepdims=True)
        total = jnp.sum(jnp.exp(tile - top), axis=0, keepdims=True)
        col_vec[:, cols] = top + jnp.log(total)

    send(col_vec, col_sib, stat_send, stat_recv, sibling)

    @pl.loop(0, 2)
    def _(n):
        @pl.when(n == 1)
        def _():
            arrived(col_sib, stat_send, stat_recv)
            from_sibling = col_sib[...]
            from_sibling = jnp.concatenate([from_sibling[:, HALF:], from_sibling[:, :HALF]], axis=1)
            col_ring[0] = lse2(col_vec[...], from_sibling)
            for k in range(1, GROUP):
                send(col_ring.at[0], col_ring.at[k], scol_send, scol_recv, text_peers[k])

        rows = pl.ds(pl.multiple_of(n * 256, 256), 256)
        tile = logits[rows, :]
        top = jnp.max(tile, axis=1, keepdims=True)
        total = jnp.sum(jnp.exp(tile - top), axis=1, keepdims=True)
        row_stat[rows, :] = jnp.broadcast_to(top + jnp.log(total), (256, 128))

    row_ring[0, 0:1, :] = jnp.transpose(row_stat[...])[0:1, :]
    for k in range(1, GROUP):
        send(row_ring.at[0], row_ring.at[k], srow_send, srow_recv, image_peers[k])

    gathered = pl.ds(0, HALF - R)
    left(images.at[gathered], ring_send.at[0], sib_recv)
    left(texts.at[gathered], ring_send.at[1], sib_recv)
    left(texts.at[pl.ds(0, HALF)], sib_send, sib_recv)
    left(col_vec, stat_send, stat_recv)

    def joined(ring):
        parts = [ring[k, 0:1, :] for k in range(GROUP)]
        top = parts[0]
        for part in parts[1:]:
            top = jnp.maximum(top, part)
        total = jnp.exp(parts[0] - top)
        for part in parts[1:]:
            total = total + jnp.exp(part - top)
        return top + jnp.log(total)

    others = pl.ds(1, GROUP - 1)
    arrived(col_ring.at[others], scol_send, scol_recv)
    col_stat[...] = joined(col_ring)
    arrived(row_ring.at[others], srow_send, srow_recv)
    row_stat[...] = jnp.transpose(jnp.broadcast_to(joined(row_ring), (128, HALF)))
    group_labels = row_ring[0, 1:2, :]
    for k in range(1, GROUP):
        group_labels = group_labels + row_ring[k, 1:2, :]
    label_stat[...] = jnp.transpose(jnp.broadcast_to(group_labels, (128, HALF)))
    left(col_ring.at[others], scol_send, scol_recv)
    left(row_ring.at[others], srow_send, srow_recv)

    @pl.loop(0, 1)
    def _(n):
        rows = pl.ds(pl.multiple_of(n * 512, 512), 512)
        at_lane = lax.broadcasted_iota(jnp.int32, (1, 2 * HALF), 1)
        member = (at_lane >> 5) & 15
        its_y, parity = member >> 1, member & 1
        its_core = jnp.where(at_lane < HALF, core, 1 - core)
        its_x = jnp.where(parity == p, x, xb)
        its_blk = (its_x * 4 + (its_y & 3)) * 2 + its_core
        its_dp = (its_y >> 2) * 8 + z
        ids = ((its_blk * 16 + its_dp) * R + (at_lane & 31)).astype(F32)
        tile = logits[rows, :]
        target = jnp.where(label_stat[rows, 0:1] == ids, 2.0, 0.0)
        both = jnp.exp(tile - row_stat[rows, 0:1]) + jnp.exp(tile - col_stat[...])
        weight = (both - target) * 0.5
        wts[rows, :] = weight.astype(BF16)
        wts_t[:, rows] = jnp.transpose(weight).astype(BF16)

    def summed(kind, piece):
        total = (grad_i if kind == 0 else grad_t)[piece_rows(kind, piece), :]
        for child in CHILDREN.get(piece, ()):
            i = index(kind, child)
            arrived(landed.at[i], rs_send.at[kind], rs_recv.at[i])
            total = total + landed[i].astype(F32)
        return total

    def pass_on(kind, piece):
        i = index(kind, piece)
        if piece in CHILDREN:
            out = stage.at[i]
            out[...] = summed(kind, piece).astype(BF16)
        else:
            out = (grad_i16 if kind == 0 else grad_t16).at[piece_rows(kind, piece)]
        send(out, landed.at[i], rs_send.at[kind], rs_recv.at[i], peer_of(kind, -parent(piece)[1]))

    def band(kind, d, start=0):
        return pl.ds(pl.multiple_of(along(place[kind], -d) * 2 * R + start, 2 * R), 2 * R)

    def parts(term, bands):
        return [(d, term[n * 2 * R : (n + 1) * 2 * R, :]) for n, d in enumerate(bands)]

    def sibling_bands(bands):
        left_side = jnp.concatenate([wts_t[band(1, d, HALF), :] for d in bands], axis=0)
        term = jnp.dot(left_side, images[...], preferred_element_type=F32)
        for d, part in parts(term, bands):
            rows = band(1, d)
            swap_out[rows, :] = part.astype(BF16)
            theirs = swap_recv.at[(d if d == 4 else -d) + 3]
            send(swap_out.at[rows], swap_in.at[rows], swap_send, theirs, sibling)

    def image_bands(bands):
        left_side = jnp.concatenate([wts[band(0, d), :] for d in bands], axis=0)
        term = jnp.dot(left_side, texts[...], preferred_element_type=F32)
        for d, part in parts(term, bands):
            grad_i[band(0, d), :] = part
            grad_i16[band(0, d), :] = part.astype(BF16)

    def text_bands(bands):
        left_side = jnp.concatenate([wts_t[band(1, d), :] for d in bands], axis=0)
        term = jnp.dot(left_side, images[...], preferred_element_type=F32)
        for d, part in parts(term, bands):
            rows = band(1, d)
            arrived(swap_in.at[rows], swap_send, swap_recv.at[d + 3])
            total = part + swap_in[rows, :].astype(F32)
            grad_t[rows, :] = total
            grad_t16[rows, :] = total.astype(BF16)

    for bands in ((4, 3, -3), (2, -2, 1, -1, 0)):
        leaves = [piece for piece in BACKWARDS if piece not in CHILDREN and piece[2] in bands]
        sibling_bands(bands)
        image_bands(bands)
        for piece in leaves:
            pass_on(0, piece)
        text_bands(bands)
        for piece in leaves:
            pass_on(1, piece)
    for piece in BACKWARDS:
        if piece in CHILDREN:
            for kind in range(2):
                pass_on(kind, piece)
    for kind, out_ref in ((0, out_image_ref), (1, out_text_ref)):
        for h in range(2):
            out_ref[pl.ds(h * H, H), :] = scale * summed(kind, (0, h, 0))

    left(swap_out, swap_send, swap_recv.at[0])
    left(grad_i16.at[gathered], rs_send.at[0], swap_recv.at[0])
    left(grad_t16.at[gathered], rs_send.at[1], swap_recv.at[0])


def per_device(image_emb, text_emb, labels, logit_scale):
    vmem = pl.BlockSpec(memory_space=pltpu.VMEM)
    smem = pl.BlockSpec(memory_space=pltpu.SMEM)
    hbm = pl.BlockSpec(memory_space=pltpu.HBM)
    dma = pltpu.SemaphoreType.DMA
    out = jax.ShapeDtypeStruct((R, E), F32)
    grads = pl.pallas_call(
        kernel,
        out_shape=(out, out),
        in_specs=[hbm, hbm, hbm, smem],
        out_specs=(vmem, vmem),
        scratch_shapes=[
            pltpu.VMEM((HALF, E), BF16),
            pltpu.VMEM((2 * HALF, E), BF16),
            pltpu.VMEM((HALF, 2 * HALF), F32),
            pltpu.VMEM((HALF, 2 * HALF), BF16),
            pltpu.VMEM((2 * HALF, HALF), BF16),
            pltpu.VMEM((HALF, E), F32),
            pltpu.VMEM((HALF, E), F32),
            pltpu.VMEM((HALF, 128), F32),
            pltpu.VMEM((1, 2 * HALF), F32),
            pltpu.VMEM((GROUP, 2, HALF), F32),
            pltpu.VMEM((1, 2 * HALF), F32),
            pltpu.VMEM((1, 2 * HALF), F32),
            pltpu.VMEM((GROUP, 1, 2 * HALF), F32),
            pltpu.VMEM((HALF, 128), F32),
            pltpu.SMEM((R,), jnp.int32),
            pltpu.VMEM((HALF, E), BF16),
            pltpu.VMEM((HALF, E), BF16),
            pltpu.VMEM((HALF, E), BF16),
            pltpu.VMEM((HALF, E), BF16),
            pltpu.VMEM((2, 2, 2, RING, H, E), BF16),
            pltpu.VMEM((2, 2, 2, RING, H, E), BF16),
            dma((3,)),
            dma((2,)), dma((2, 2, 2, RING)),
            dma(()), dma(()),
            dma(()), dma(()),
            dma(()), dma(()),
            dma(()), dma(()),
            dma(()), dma((RING,)),
            dma((2,)), dma((2, 2, 2, RING)),
        ],
        compiler_params=pltpu.CompilerParams(
            collective_id=0, has_side_effects=True, vmem_limit_bytes=56 * 1024 * 1024
        ),
        cost_estimate=pl.CostEstimate(flops=3221225472, bytes_accessed=262144, transcendentals=2097152),
        name="contrastive",
    )(image_emb, text_emb, labels, logit_scale.reshape(1))
    return tuple(grad.astype(BF16) for grad in grads)


def solution(mesh):
    in_specs = (P(("blk", "dp"), None), P(("blk", "dp"), None), P(("blk", "dp")), P())
    out_specs = (P(("blk", "dp"), None), P(("blk", "dp"), None))
    return jax.shard_map(
        per_device, mesh=mesh, in_specs=in_specs, out_specs=out_specs, check_vma=False
    )
```
